32 devices in a mesh: seq: 16 (over z, y, x), chan: 2 (over core).
Axes of the slice: x: 2, y: 2, z: 4, core: 2. Of those that a mesh axis runs over, the one named last changes fastest.
Arguments:
- hidden_in: bfloat16 [2048, 8192], P('seq', 'chan'), as said below
- query_mr: bfloat16 [2048, 8192], P('seq', 'chan'), may hold values from -6 to 6
- key_mr: bfloat16 [2048, 8192], P('seq', 'chan'), may hold values from -6 to 6
- value_mr: bfloat16 [2048, 8192], P('seq', 'chan'), may hold values from -6 to 6
- query_li: bfloat16 [2048, 8192], P('seq', 'chan'), may hold values from -6 to 6
- key_li: bfloat16 [2048, 8192], P('seq', 'chan'), may hold values from -6 to 6
- mr_filter: bfloat16 [128, 512], P(None, 'chan'), may hold values from -0.5 to 0.5
- li_rate: float32 [16, 8192], P(None, 'chan'), as said below
- li_residue: float32 [16, 8192], P(None, 'chan'), may hold values from -4 to 4
- norm_gain: float32 [8192], P('chan'), may hold values from 0.25 to 1.75
Outputs:
- normed_out: bfloat16 [2048, 8192], P('seq', 'chan')
The draws below stay inside these ranges and needn't reach their ends.
Inputs may be any that keep to these rules, and one draw needn't show every extreme that they name: `hidden_in`: real values of moderate size. `li_rate`: decay rates per position, all positive, from 1 / 20480 to 1 / 30.
All inputs are finite; a program needn't handle non-finite values.
Results may differ from the reference program's by a relative error of at most 0.0055.
Values may be sent and summed in bfloat16 or wider, within the bound.
A program may use at most 128 MiB of HBM per device.

```python
import math
import jax
import jax.numpy as jnp
from jax import lax

D = 8192
MR_LEN = 128
POLES = 16
TOKENS = 2048
MR_GROUPS = 512


def draw_hidden_in(key, part):
    key = jax.random.fold_in(key, 11)
    key_base, key_rows, key_cols = jax.random.split(key, 3)
    column_pos = jnp.arange(D).astype(jnp.float32) / (D - 1)
    row_scale = jnp.exp(jax.random.uniform(key_rows, (TOKENS, 1), jnp.float32, math.log(0.4), math.log(2.5)))
    base_vals = jax.random.normal(key_base, (TOKENS, D), jnp.float32)
    col_scale = jnp.exp(math.log(3.0) * column_pos + jax.random.uniform(key_cols, (D,), jnp.float32, math.log(0.4), math.log(2.5)))
    return (base_vals * row_scale * col_scale[None, :]).astype(jnp.bfloat16)


def draw_li_rate(key, part):
    key = jax.random.fold_in(key, 23)
    key_pick, key_value = jax.random.split(key, 2)
    slow_share = 0.5
    is_slow = jax.random.uniform(key_pick, (POLES, D), jnp.float32) < slow_share
    uniform_vals = jax.random.uniform(key_value, (POLES, D), jnp.float32)
    slow_low = math.log(0.1 / TOKENS)
    slow_high = math.log(2.0 / TOKENS)
    fast_high = math.log(1.0 / 30.0)
    slow_rate = jnp.exp(slow_low + uniform_vals * (slow_high - slow_low))
    fast_rate = jnp.exp(slow_high + uniform_vals * (fast_high - slow_high))
    return jnp.where(is_slow, slow_rate, fast_rate).astype(jnp.float32)


def shard_levels(own_key, dims, cuts, smallest, high):
    level, own = 1.0, jax.random.fold_in(own_key, 6)
    for axis_at, blocks in cuts:
        heights = jnp.exp(jax.random.uniform(jax.random.fold_in(own, axis_at), (blocks,), jnp.float32, smallest / len(cuts), high / len(cuts)))
        level = level * jnp.repeat(heights, dims[axis_at] // blocks).reshape([-1 if axis == axis_at else 1 for axis in range(len(dims))])
    return level


def gaussian(key, dims, deviation, most, pieces=(), held_as=jnp.bfloat16):
    gain = shard_levels(key, dims, pieces, -0.22, 0.18) if pieces else 1.0
    values = jax.random.normal(key, dims, jnp.float32) * deviation * gain
    return jnp.minimum(jnp.maximum(values, -most), most).astype(held_as)


def setup_inputs(seed: int = 0) -> dict:
    seeds = jax.random.split(jax.random.key(seed), 11)
    hidden_in = draw_hidden_in(jax.random.fold_in(seeds[10], 71), 0)
    query_mr = gaussian(seeds[1], (TOKENS, D), 1.0, 6.0, ((0, 16), (1, 2)))
    key_mr = gaussian(seeds[2], (TOKENS, D), 1.0, 6.0, ((0, 16), (1, 2)))
    value_mr = gaussian(seeds[3], (TOKENS, D), 1.0, 6.0, ((0, 16), (1, 2)))
    query_li = gaussian(seeds[4], (TOKENS, D), 1.0, 6.0, ((0, 16), (1, 2)))
    key_li = gaussian(seeds[5], (TOKENS, D), 1.0, 6.0, ((0, 16), (1, 2)))
    mr_filter = gaussian(seeds[6], (MR_LEN, MR_GROUPS), MR_LEN ** -0.5, 0.5, ((1, 2),))
    li_rate = draw_li_rate(jax.random.fold_in(seeds[10], 71), 0)
    li_residue = gaussian(seeds[8], (POLES, D), 0.25, 4.0, ((1, 2),), jnp.float32)
    norm_gain = jnp.clip(1.0 + 0.15 * jax.random.normal(seeds[9], (D,), jnp.float32), 0.25, 1.75)
    return {"hidden_in": hidden_in, "query_mr": query_mr, "key_mr": key_mr, "value_mr": value_mr, "query_li": query_li, "key_li": key_li, "mr_filter": mr_filter, "li_rate": li_rate, "li_residue": li_residue, "norm_gain": norm_gain}


def toeplitz_band(filter_taps, filter_len):
    group_count = filter_taps.shape[1]
    padded = jnp.concatenate([jnp.zeros((1, group_count), filter_taps.dtype), jnp.flip(filter_taps, 0), jnp.zeros((filter_len, group_count), filter_taps.dtype)], 0)
    repeated = jnp.tile(padded, (filter_len, 1))[:filter_len * 2 * filter_len]
    return repeated.reshape(filter_len, 2 * filter_len, group_count)

def medium_conv(product, mr_filter):
    tokens, channels = product.shape
    filter_len = mr_filter.shape[0]
    group_count = mr_filter.shape[1]
    toeplitz = toeplitz_band(mr_filter.astype(jnp.float32), filter_len)
    padded = jnp.concatenate([jnp.zeros((filter_len, channels), jnp.bfloat16), product], 0)
    blocks = tokens // filter_len
    earlier_rows = padded[:-filter_len].reshape(blocks, filter_len, group_count, channels // group_count)
    latter_rows = padded[filter_len:].reshape(blocks, filter_len, group_count, channels // group_count)

    def one_block(block_index):
        window = jnp.concatenate([earlier_rows[block_index], latter_rows[block_index]], 0).astype(jnp.float32)
        return jnp.einsum('tsg,sgk->tgk', toeplitz, window, precision=lax.Precision.HIGHEST)
    result = lax.map(one_block, jnp.arange(blocks))
    return result.reshape(tokens, channels)

def long_conv(source, li_rate, li_residue):
    block_len = 16
    tokens, channels = source.shape
    pole_count = li_rate.shape[0]
    scaled = li_residue * jnp.sqrt(-jnp.expm1(-2.0 * li_rate))
    lag_steps = jnp.arange(block_len).astype(jnp.float32)
    mode_taps = lax.optimization_barrier(jnp.sum(scaled[None] * jnp.exp(-lag_steps[:, None, None] * li_rate[None]), 1))
    lag_index = jnp.arange(block_len).astype(jnp.int32)
    lag_grid = lag_index[:, None] - lag_index[None, :]
    selector = (lag_grid[:, :, None] == lag_index[None, None, :]).astype(jnp.float32)
    intra_block = jnp.einsum('tsd,dc->tsc', selector, mode_taps, precision=lax.Precision.HIGHEST)
    decay_out = jnp.exp(-(block_len - 1 - lag_steps)[:, None, None] * li_rate[None])
    decay_in = scaled[None] * jnp.exp(-(lag_steps + 1.0)[:, None, None] * li_rate[None])
    block_decay = jnp.exp(-block_len * li_rate)
    blocks_in = source.reshape(tokens // block_len, block_len, channels)

    def advance(state, block_rows):
        local_part = jnp.einsum('tsc,sc->tc', intra_block, block_rows, precision=lax.Precision.HIGHEST)
        from_states = jnp.einsum('tnc,nc->tc', decay_in, state, precision=lax.Precision.HIGHEST)
        new_state = block_decay * state + jnp.einsum('snc,sc->nc', decay_out, block_rows, precision=lax.Precision.HIGHEST)
        return (new_state, local_part + from_states)
    _, outputs = lax.scan(advance, jnp.zeros((pole_count, channels), jnp.float32), blocks_in)
    return outputs.reshape(tokens, channels)

def reference(hidden_in, query_mr, key_mr, value_mr, query_li, key_li, mr_filter, li_rate, li_residue, norm_gain):
    product = (key_mr.astype(jnp.float32) * value_mr.astype(jnp.float32)).astype(jnp.bfloat16)
    conv_mr = medium_conv(product, mr_filter)
    out_mr = (query_mr.astype(jnp.float32) * conv_mr).astype(jnp.bfloat16)
    source = key_li.astype(jnp.float32) * out_mr.astype(jnp.float32)
    conv_li = long_conv(source, li_rate, li_residue)
    combined = hidden_in.astype(jnp.float32) + out_mr.astype(jnp.float32) + query_li.astype(jnp.float32) * conv_li
    inverse_rms = lax.rsqrt(lax.optimization_barrier(jnp.mean(combined * combined, axis=1, keepdims=True)) + 1e-06)
    return (combined * inverse_rms * norm_gain[None, :]).astype(jnp.bfloat16)
```

```python
import functools

import jax
import jax.numpy as jnp
from jax import lax
from jax.experimental import pallas as pl
from jax.experimental.pallas import tpu as pltpu
from jax.sharding import PartitionSpec as P

LANES = 128
SUBS = 8
CHUNK = LANES * SUBS
f32 = jnp.float32
bf16 = jnp.bfloat16


def mixer_kernel(
    seq_n, chan_n, chunks, group_width,
    hid_h, qmr_h, kmr_h, vmr_h, qli_h, kli_h, filt_h, rate_h, resid_h, gain_h,
    out_h,
    hid, qmr, kmr, vmr, qli, kli, filt, rate_in, resid_in, ngain,
    prod, halo, outb, taps, upper, acc, src, rate, mgain,
    prefix, total, state_out, state_in, squares_out, squares_in,
    in_sem, par_sem, out_sem, halo_send, halo_recv,
    st_send, st_recv, sq_send, sq_recv,
):
    pos = lax.axis_index("seq")
    lane_pos = lax.axis_index("chan")
    tokens = hid.shape[1]
    modes = rate_in.shape[0]
    slab = modes * SUBS
    rounds = seq_n.bit_length() - 1
    per_block = LANES // group_width
    nxt = lax.rem(pos + 1, seq_n)
    prv = lax.rem(pos + seq_n - 1, seq_n)

    def cols(k):
        return pl.ds(k * CHUNK, CHUNK)

    pairs = ((kmr_h, kmr), (vmr_h, vmr), (qmr_h, qmr), (kli_h, kli), (hid_h, hid), (qli_h, qli))

    def in_copy(a, k):
        return pltpu.make_async_copy(pairs[a][0].at[:, cols(k)], pairs[a][1].at[k], in_sem.at[a, k])

    par_copies = [
        pltpu.make_async_copy(h, v, par_sem.at[i])
        for i, (h, v) in enumerate(
            ((filt_h, filt), (rate_h, rate_in), (resid_h, resid_in), (gain_h, ngain))
        )
    ]
    for k in range(chunks):
        in_copy(0, k).start()
        in_copy(1, k).start()
    for c in par_copies:
        c.start()
    for a in range(2, 6):
        for k in range(chunks):
            in_copy(a, k).start()

    barrier = pltpu.get_barrier_semaphore()

    def greet(ids):
        pl.semaphore_signal(barrier, inc=1, device_id=ids, device_id_type=pl.DeviceIdType.MESH)

    greet({"seq": nxt})
    greet({"seq": prv})
    bits = [lax.rem(pos // (1 << r), 2) for r in range(rounds)]
    partners = [pos + (1 << r) * (1 - 2 * bits[r]) for r in range(rounds)]
    for r in range(rounds):
        greet({"seq": partners[r]})
    for d in range(1, chan_n):
        greet({"chan": lax.rem(lane_pos + d, chan_n)})

    def halo_copy(k):
        return pltpu.make_async_remote_copy(
            src_ref=prod.at[k], dst_ref=halo.at[k],
            send_sem=halo_send.at[k], recv_sem=halo_recv.at[k],
            device_id={"seq": nxt}, device_id_type=pl.DeviceIdType.MESH,
        )

    def state_copy(r, k):
        return pltpu.make_async_remote_copy(
            src_ref=state_out.at[r, k], dst_ref=state_in.at[r, k],
            send_sem=st_send.at[r, k], recv_sem=st_recv.at[r, k],
            device_id={"seq": partners[r]}, device_id_type=pl.DeviceIdType.MESH,
        )

    def squares_copy(d):
        return pltpu.make_async_remote_copy(
            src_ref=squares_out, dst_ref=squares_in.at[d - 1],
            send_sem=sq_send.at[d - 1], recv_sem=sq_recv.at[d - 1],
            device_id={"chan": lax.rem(lane_pos + d, chan_n)},
            device_id_type=pl.DeviceIdType.MESH,
        )

    @pl.when(pos == 0)
    def _():
        halo[...] = jnp.zeros_like(halo)

    for k in range(chunks):
        in_copy(0, k).wait()
        in_copy(1, k).wait()
        prod[k] = (kmr[k].astype(f32) * vmr[k].astype(f32)).astype(bf16)
        if k == 0:
            pl.semaphore_wait(barrier, 2 + rounds + chan_n - 1)

        @pl.when(pos < seq_n - 1)
        def _():
            halo_copy(k).start()

    for c in par_copies:
        c.wait()

    tap_i = lax.broadcasted_iota(jnp.int32, (tokens, tokens), 0)
    pos_i = lax.broadcasted_iota(jnp.int32, (tokens, tokens), 1)
    wrap = jnp.where(lax.rem(tap_i + pos_i, tokens) == 0, 1.0, 0.0).astype(bf16)
    taps[...] = lax.dot_general(
        filt[...], wrap, (((0,), (0,)), ((), ())), preferred_element_type=f32
    )

    for k in range(chunks):
        for b in range(SUBS):
            lanes = pl.ds(k * CHUNK + b * LANES, LANES)
            r = rate_in[:, lanes]
            x = 2.0 * r
            series = x * (
                1.0 - x * (1 / 2) * (1.0 - x * (1 / 3) * (1.0 - x * (1 / 4) * (
                    1.0 - x * (1 / 5) * (1.0 - x * (1 / 6) * (1.0 - x * (1 / 7))))))
            )
            grown = jnp.where(x < 0.1, series, 1.0 - jnp.exp(-x))
            rows = pl.ds(k * slab + b, modes, stride=SUBS)
            rate[rows, :] = r
            mgain[rows, :] = resid_in[:, lanes] * jnp.sqrt(grown)

    def spread(x):
        lane = lax.broadcasted_iota(jnp.int32, x.shape, 1)
        wide = x.astype(f32)
        return jnp.concatenate(
            [
                jnp.where(lane // group_width == g, wide, 0.0).astype(bf16)
                for g in range(per_block)
            ],
            0,
        )

    row_i = lax.broadcasted_iota(jnp.int32, (tokens, LANES), 0)
    lane_i = lax.broadcasted_iota(jnp.int32, (tokens, LANES), 1)
    lower_mask = lane_i <= row_i

    for k in range(chunks):

        def local_block(b, carry):
            j = k * SUBS + b
            lanes = pl.ds(pl.multiple_of(b * LANES, LANES), LANES)
            rows = taps[pl.ds(pl.multiple_of(j * per_block, per_block), per_block), :]
            lows, ups = [], []
            for g in range(per_block):
                ring = pltpu.roll(
                    jnp.broadcast_to(rows[g : g + 1, :], (tokens, LANES)),
                    0, 1, stride=1, stride_axis=0,
                )
                lows.append(jnp.where(lower_mask, ring, 0.0).astype(bf16))
                ups.append(jnp.where(lower_mask, 0.0, ring).astype(bf16))
            upper[j] = jnp.concatenate(ups, 1)
            acc[k, :, lanes] = jnp.dot(
                jnp.concatenate(lows, 1), spread(prod[k, :, lanes]), preferred_element_type=f32
            )
            return carry

        lax.fori_loop(0, SUBS, local_block, 0)

    def chunk_rate(k):
        return rate[pl.ds(k * slab, slab), :]

    def chunk_mode(ref, k, n):
        return ref[pl.ds(k * slab + n * SUBS, SUBS), :]

    def medium_and_states(k):
        @pl.when(pos > 0)
        def _():
            halo_copy(k).wait_recv()

        for a in range(2, 5):
            in_copy(a, k).wait()

        def block(b, carry):
            j = k * SUBS + b
            lanes = pl.ds(pl.multiple_of(b * LANES, LANES), LANES)
            conv = acc[k, :, lanes] + jnp.dot(
                upper[j], spread(halo[k, :, lanes]), preferred_element_type=f32
            )
            out_mr = (qmr[k, :, lanes].astype(f32) * conv).astype(bf16).astype(f32)
            src[pl.ds(pl.multiple_of(j * tokens, tokens), tokens), :] = (
                kli[k, :, lanes].astype(f32) * out_mr
            )
            acc[k, :, lanes] = hid[k, :, lanes].astype(f32) + out_mr
            return carry

        lax.fori_loop(0, SUBS, block, 0)

        decay = [jnp.exp(-chunk_mode(rate, k, n)) for n in range(modes)]
        gain = [chunk_mode(mgain, k, n) for n in range(modes)]

        def step(t, states):
            at = pl.ds(k * SUBS * tokens + t, SUBS, stride=tokens)
            x = src[at, :]
            states = tuple(decay[n] * states[n] + x for n in range(modes))
            parts = [gain[n] * states[n] for n in range(modes)]
            while len(parts) > 1:
                parts = [a + b for a, b in zip(parts[::2], parts[1::2])]
            src[at, :] = parts[0]
            return states

        zero = jnp.zeros((SUBS, LANES), f32)
        states = lax.fori_loop(0, tokens, step, (zero,) * modes, unroll=4)
        for n in range(modes):
            total[k, pl.ds(n * SUBS, SUBS), :] = states[n]
        prefix[k] = jnp.zeros((slab, LANES), f32)

    def send_state(r, k):
        def go():
            state_out[r, k] = total[k].astype(bf16)
            state_copy(r, k).start()

        if r < rounds - 1:
            go()
        else:
            pl.when(bits[r] == 0)(go)

    def take_state(r, k):
        span = 1 << r
        if r < rounds - 1:
            state_copy(r, k).wait_recv()
            got = state_in[r, k].astype(f32)
            rates = chunk_rate(k)
            whole = jnp.exp(rates * (-1.0 * tokens * span))
            upper_half = bits[r] == 1
            ahead = (tokens * lax.rem(pos, span)).astype(f32)
            weight = jnp.exp(-rates * ahead)
            mine = total[k]
            prefix[k] = prefix[k] + jnp.where(upper_half, weight * got, 0.0)
            total[k] = jnp.where(upper_half, whole * got + mine, whole * mine + got)
        else:

            @pl.when(bits[r] == 1)
            def _():
                state_copy(r, k).wait_recv()
                got = state_in[r, k].astype(f32)
                ahead = (tokens * lax.rem(pos, span)).astype(f32)
                prefix[k] = prefix[k] + jnp.exp(-chunk_rate(k) * ahead) * got

    def finish_chunk(k):
        decay = [jnp.exp(-chunk_mode(rate, k, n)) for n in range(modes)]
        start = tuple(
            chunk_mode(mgain, k, n) * prefix[k, pl.ds(n * SUBS, SUBS), :] for n in range(modes)
        )

        def step(t, waves):
            at = pl.ds(k * SUBS * tokens + t, SUBS, stride=tokens)
            waves = tuple(decay[n] * waves[n] for n in range(modes))
            parts = list(waves)
            while len(parts) > 1:
                parts = [a + b for a, b in zip(parts[::2], parts[1::2])]
            src[at, :] = src[at, :] + parts[0]
            return waves

        lax.fori_loop(0, tokens, step, start, unroll=4)
        in_copy(5, k).wait()

        def block(b, carry):
            j = k * SUBS + b
            lanes = pl.ds(pl.multiple_of(b * LANES, LANES), LANES)
            conv = src[pl.ds(pl.multiple_of(j * tokens, tokens), tokens), :]
            combined = acc[k, :, lanes] + qli[k, :, lanes].astype(f32) * conv
            acc[k, :, lanes] = combined
            squares_out[...] += combined * combined
            return carry

        lax.fori_loop(0, SUBS, block, 0)

    squares_out[...] = jnp.zeros_like(squares_out)
    for turn in range(chunks + rounds):
        for k in range(chunks):
            r = turn - k - 1
            if 0 <= r < rounds:
                take_state(r, k)
                if r + 1 < rounds:
                    send_state(r + 1, k)
        if turn < chunks:
            medium_and_states(turn)
            send_state(0, turn)
        done = turn - rounds
        if 0 <= done < chunks:
            finish_chunk(done)

    sums = squares_out[...]
    for d in range(1, chan_n):
        squares_copy(d).start()
    for d in range(1, chan_n):
        squares_copy(d).wait_recv()
        sums = sums + squares_in[d - 1]
    width = chunks * CHUNK * chan_n
    inverse = lax.rsqrt(jnp.sum(sums, 1, keepdims=True) / width + 1e-06)

    for k in range(chunks):
        outb[k] = (acc[k] * inverse * ngain[:, cols(k)]).astype(bf16)
        pltpu.make_async_copy(outb.at[k], out_h.at[:, cols(k)], out_sem.at[k]).start()

    for k in range(chunks):
        pltpu.make_async_copy(outb.at[k], out_h.at[:, cols(k)], out_sem.at[k]).wait()

        @pl.when(pos < seq_n - 1)
        def _():
            halo_copy(k).wait_send()

        for r in range(rounds - 1):
            state_copy(r, k).wait_send()

        @pl.when(bits[rounds - 1] == 0)
        def _():
            state_copy(rounds - 1, k).wait_send()

    for d in range(1, chan_n):
        squares_copy(d).wait_send()


def per_device(
    seq_n, chan_n,
    hidden_in, query_mr, key_mr, value_mr, query_li, key_li,
    mr_filter, li_rate, li_residue, norm_gain,
):
    tokens, channels = hidden_in.shape
    groups = mr_filter.shape[1]
    modes = li_rate.shape[0]
    chunks = channels // CHUNK
    rounds = seq_n.bit_length() - 1
    slab = modes * SUBS
    assert seq_n == 1 << rounds and tokens == mr_filter.shape[0] == LANES
    big = pltpu.VMEM((chunks, tokens, CHUNK), bf16)
    dma = pltpu.SemaphoreType.DMA
    return pl.pallas_call(
        functools.partial(mixer_kernel, seq_n, chan_n, chunks, channels // groups),
        out_shape=jax.ShapeDtypeStruct((tokens, channels), bf16),
        in_specs=[pl.BlockSpec(memory_space=pl.ANY)] * 10,
        out_specs=pl.BlockSpec(memory_space=pl.ANY),
        scratch_shapes=[
            big, big, big, big, big, big,
            pltpu.VMEM(mr_filter.shape, bf16),
            pltpu.VMEM(li_rate.shape, f32),
            pltpu.VMEM(li_residue.shape, f32),
            pltpu.VMEM((1, channels), f32),
            big, big, big,
            pltpu.VMEM((groups, tokens), f32),
            pltpu.VMEM((channels // LANES, tokens, tokens * LANES * groups // channels), bf16),
            pltpu.VMEM((chunks, tokens, CHUNK), f32),
            pltpu.VMEM((channels // LANES * tokens, LANES), f32),
            pltpu.VMEM((chunks * slab, LANES), f32),
            pltpu.VMEM((chunks * slab, LANES), f32),
            pltpu.VMEM((chunks, slab, LANES), f32),
            pltpu.VMEM((chunks, slab, LANES), f32),
            pltpu.VMEM((rounds, chunks, slab, LANES), bf16),
            pltpu.VMEM((rounds, chunks, slab, LANES), bf16),
            pltpu.VMEM((tokens, LANES), f32),
            pltpu.VMEM((max(chan_n - 1, 1), tokens, LANES), f32),
            dma((6, chunks)),
            dma((4,)),
            dma((chunks,)),
            dma((chunks,)),
            dma((chunks,)),
            dma((rounds, chunks)),
            dma((rounds, chunks)),
            dma((max(chan_n - 1, 1),)),
            dma((max(chan_n - 1, 1),)),
        ],
        compiler_params=pltpu.CompilerParams(
            collective_id=0, has_side_effects=True, vmem_limit_bytes=48 * 1024 * 1024
        ),
        cost_estimate=pl.CostEstimate(
            flops=4 * tokens * tokens * channels * LANES * groups // channels,
            bytes_accessed=14 * tokens * channels,
            transcendentals=4 * modes * channels,
        ),
        name="hyena_mixers",
    )(
        hidden_in, query_mr, key_mr, value_mr, query_li, key_li,
        mr_filter, li_rate, li_residue, norm_gain.reshape(1, channels),
    )


def solution(mesh):
    seq_n, chan_n = mesh.shape["seq"], mesh.shape["chan"]
    rows = P("seq", "chan")
    by_channel = P(None, "chan")
    in_specs = (rows,) * 6 + (by_channel,) * 3 + (P("chan"),)
    return jax.shard_map(
        functools.partial(per_device, seq_n, chan_n),
        mesh=mesh, in_specs=in_specs, out_specs=rows, check_vma=False,
    )
```

```python
import functools

import jax
import jax.numpy as jnp
from jax import lax
from jax.experimental import pallas as pl
from jax.experimental.pallas import tpu as pltpu
from jax.sharding import PartitionSpec as P

LANES = 128
SUBS = 8
CHUNK = LANES * SUBS
f32 = jnp.float32
bf16 = jnp.bfloat16


def mixer_kernel(
    seq_n, chan_n, chunks, group_width,
    hid_h, qmr_h, kmr_h, vmr_h, qli_h, kli_h, filt_h, rate_h, resid_h, gain_h,
    out_h,
    hid, qmr, kmr, vmr, qli, kli, filt, rate_in, resid_in, ngain,
    prod, halo, outb, taps, upper, acc, src, rate, mgain,
    prefix, total, state_out, state_in, squares_out, squares_in,
    in_sem, par_sem, out_sem, halo_send, halo_recv,
    st_send, st_recv, sq_send, sq_recv,
):
    pos = lax.axis_index("seq")
    lane_pos = lax.axis_index("chan")
    tokens = hid.shape[1]
    modes = rate_in.shape[0]
    slab = modes * SUBS
    rounds = seq_n.bit_length() - 1
    per_block = LANES // group_width
    nxt = lax.rem(pos + 1, seq_n)
    prv = lax.rem(pos + seq_n - 1, seq_n)

    def cols(k):
        return pl.ds(k * CHUNK, CHUNK)

    pairs = ((kmr_h, kmr), (vmr_h, vmr), (qmr_h, qmr), (kli_h, kli), (hid_h, hid), (qli_h, qli))

    def in_copy(a, k):
        return pltpu.make_async_copy(pairs[a][0].at[:, cols(k)], pairs[a][1].at[k], in_sem.at[a, k])

    par_copies = [
        pltpu.make_async_copy(h, v, par_sem.at[i])
        for i, (h, v) in enumerate(
            ((filt_h, filt), (rate_h, rate_in), (resid_h, resid_in), (gain_h, ngain))
        )
    ]
    for k in range(chunks):
        in_copy(0, k).start()
        in_copy(1, k).start()
    for c in par_copies:
        c.start()
    for a in range(2, 6):
        for k in range(chunks):
            in_copy(a, k).start()

    barrier = pltpu.get_barrier_semaphore()

    def greet(ids):
        pl.semaphore_signal(barrier, inc=1, device_id=ids, device_id_type=pl.DeviceIdType.MESH)

    greet({"seq": nxt})
    greet({"seq": prv})
    bits = [lax.rem(pos // (1 << r), 2) for r in range(rounds)]
    partners = [pos + (1 << r) * (1 - 2 * bits[r]) for r in range(rounds)]
    for r in range(rounds):
        greet({"seq": partners[r]})
    for d in range(1, chan_n):
        greet({"chan": lax.rem(lane_pos + d, chan_n)})

    def halo_copy(k):
        return pltpu.make_async_remote_copy(
            src_ref=prod.at[k], dst_ref=halo.at[k],
            send_sem=halo_send.at[k], recv_sem=halo_recv.at[k],
            device_id={"seq": nxt}, device_id_type=pl.DeviceIdType.MESH,
        )

    def state_copy(r, k):
        return pltpu.make_async_remote_copy(
            src_ref=state_out.at[r, k], dst_ref=state_in.at[r, k],
            send_sem=st_send.at[r, k], recv_sem=st_recv.at[r, k],
            device_id={"seq": partners[r]}, device_id_type=pl.DeviceIdType.MESH,
        )

    def squares_copy(d):
        return pltpu.make_async_remote_copy(
            src_ref=squares_out, dst_ref=squares_in.at[d - 1],
            send_sem=sq_send.at[d - 1], recv_sem=sq_recv.at[d - 1],
            device_id={"chan": lax.rem(lane_pos + d, chan_n)},
            device_id_type=pl.DeviceIdType.MESH,
        )

    @pl.when(pos == 0)
    def _():
        halo[...] = jnp.zeros_like(halo)

    for k in range(chunks):
        in_copy(0, k).wait()
        in_copy(1, k).wait()
        prod[k] = (kmr[k].astype(f32) * vmr[k].astype(f32)).astype(bf16)
        if k == 0:
            pl.semaphore_wait(barrier, 2 + rounds + chan_n - 1)

        @pl.when(pos < seq_n - 1)
        def _():
            halo_copy(k).start()

    for c in par_copies:
        c.wait()

    tap_i = lax.broadcasted_iota(jnp.int32, (tokens, tokens), 0)
    pos_i = lax.broadcasted_iota(jnp.int32, (tokens, tokens), 1)
    wrap = jnp.where(lax.rem(tap_i + pos_i, tokens) == 0, 1.0, 0.0).astype(bf16)
    taps[...] = lax.dot_general(
        filt[...], wrap, (((0,), (0,)), ((), ())), preferred_element_type=f32
    )

    for k in range(chunks):
        for b in range(SUBS):
            lanes = pl.ds(k * CHUNK + b * LANES, LANES)
            r = rate_in[:, lanes]
            x = 2.0 * r
            series = x * (
                1.0 - x * (1 / 2) * (1.0 - x * (1 / 3) * (1.0 - x * (1 / 4) * (
                    1.0 - x * (1 / 5) * (1.0 - x * (1 / 6) * (1.0 - x * (1 / 7))))))
            )
            grown = jnp.where(x < 0.1, series, 1.0 - jnp.exp(-x))
            rows = pl.ds(k * slab + b, modes, stride=SUBS)
            rate[rows, :] = r
            mgain[rows, :] = resid_in[:, lanes] * jnp.sqrt(grown)

    def spread(x):
        lane = lax.broadcasted_iota(jnp.int32, x.shape, 1)
        wide = x.astype(f32)
        return jnp.concatenate(
            [
                jnp.where(lane // group_width == g, wide, 0.0).astype(bf16)
                for g in range(per_block)
            ],
            0,
        )

    row_i = lax.broadcasted_iota(jnp.int32, (tokens, LANES), 0)
    lane_i = lax.broadcasted_iota(jnp.int32, (tokens, LANES), 1)
    lower_mask = lane_i <= row_i

    for k in range(chunks):

        def local_block(b, carry):
            j = k * SUBS + b
            lanes = pl.ds(pl.multiple_of(b * LANES, LANES), LANES)
            rows = taps[pl.ds(pl.multiple_of(j * per_block, per_block), per_block), :]
            lows, ups = [], []
            for g in range(per_block):
                ring = pltpu.roll(
                    jnp.broadcast_to(rows[g : g + 1, :], (tokens, LANES)),
                    0, 1, stride=1, stride_axis=0,
                )
                lows.append(jnp.where(lower_mask, ring, 0.0).astype(bf16))
                ups.append(jnp.where(lower_mask, 0.0, ring).astype(bf16))
            upper[j] = jnp.concatenate(ups, 1)
            acc[k, :, lanes] = jnp.dot(
                jnp.concatenate(lows, 1), spread(prod[k, :, lanes]), preferred_element_type=f32
            )
            return carry

        lax.fori_loop(0, SUBS, local_block, 0)

    def chunk_rate(k):
        return rate[pl.ds(k * slab, slab), :]

    def chunk_mode(ref, k, n):
        return ref[pl.ds(k * slab + n * SUBS, SUBS), :]

    def medium_and_states(k):
        @pl.when(pos > 0)
        def _():
            halo_copy(k).wait_recv()

        for a in range(2, 5):
            in_copy(a, k).wait()

        def block(b, carry):
            j = k * SUBS + b
            lanes = pl.ds(pl.multiple_of(b * LANES, LANES), LANES)
            conv = acc[k, :, lanes] + jnp.dot(
                upper[j], spread(halo[k, :, lanes]), preferred_element_type=f32
            )
            out_mr = (qmr[k, :, lanes].astype(f32) * conv).astype(bf16).astype(f32)
            src[pl.ds(pl.multiple_of(j * tokens, tokens), tokens), :] = (
                kli[k, :, lanes].astype(f32) * out_mr
            )
            acc[k, :, lanes] = hid[k, :, lanes].astype(f32) + out_mr
            return carry

        lax.fori_loop(0, SUBS, block, 0)

        decay = [jnp.exp(-chunk_mode(rate, k, n)) for n in range(modes)]
        gain = [chunk_mode(mgain, k, n) for n in range(modes)]

        def step(t, states):
            at = pl.ds(k * SUBS * tokens + t, SUBS, stride=tokens)
            x = src[at, :]
            states = tuple(decay[n] * states[n] + x for n in range(modes))
            parts = [gain[n] * states[n] for n in range(modes)]
            while len(parts) > 1:
                parts = [a + b for a, b in zip(parts[::2], parts[1::2])]
            src[at, :] = parts[0]
            return states

        zero = jnp.zeros((SUBS, LANES), f32)
        states = lax.fori_loop(0, tokens, step, (zero,) * modes, unroll=16)
        for n in range(modes):
            total[k, pl.ds(n * SUBS, SUBS), :] = states[n]
        prefix[k] = jnp.zeros((slab, LANES), f32)

    def send_state(r, k):
        def go():
            state_out[r, k] = total[k].astype(bf16)
            state_copy(r, k).start()

        if r < rounds - 1:
            go()
        else:
            pl.when(bits[r] == 0)(go)

    def take_state(r, k):
        span = 1 << r
        if r < rounds - 1:
            state_copy(r, k).wait_recv()
            got = state_in[r, k].astype(f32)
            rates = chunk_rate(k)
            whole = jnp.exp(rates * (-1.0 * tokens * span))
            upper_half = bits[r] == 1
            ahead = (tokens * lax.rem(pos, span)).astype(f32)
            weight = jnp.exp(-rates * ahead)
            mine = total[k]
            prefix[k] = prefix[k] + jnp.where(upper_half, weight * got, 0.0)
            total[k] = jnp.where(upper_half, whole * got + mine, whole * mine + got)
        else:

            @pl.when(bits[r] == 1)
            def _():
                state_copy(r, k).wait_recv()
                got = state_in[r, k].astype(f32)
                ahead = (tokens * lax.rem(pos, span)).astype(f32)
                prefix[k] = prefix[k] + jnp.exp(-chunk_rate(k) * ahead) * got

    def finish_chunk(k):
        decay = [jnp.exp(-chunk_mode(rate, k, n)) for n in range(modes)]
        start = tuple(
            chunk_mode(mgain, k, n) * prefix[k, pl.ds(n * SUBS, SUBS), :] for n in range(modes)
        )

        def step(t, waves):
            at = pl.ds(k * SUBS * tokens + t, SUBS, stride=tokens)
            waves = tuple(decay[n] * waves[n] for n in range(modes))
            parts = list(waves)
            while len(parts) > 1:
                parts = [a + b for a, b in zip(parts[::2], parts[1::2])]
            src[at, :] = src[at, :] + parts[0]
            return waves

        lax.fori_loop(0, tokens, step, start, unroll=16)
        in_copy(5, k).wait()

        def block(b, carry):
            j = k * SUBS + b
            lanes = pl.ds(pl.multiple_of(b * LANES, LANES), LANES)
            conv = src[pl.ds(pl.multiple_of(j * tokens, tokens), tokens), :]
            combined = acc[k, :, lanes] + qli[k, :, lanes].astype(f32) * conv
            acc[k, :, lanes] = combined
            squares_out[...] += combined * combined
            return carry

        lax.fori_loop(0, SUBS, block, 0)

    squares_out[...] = jnp.zeros_like(squares_out)
    for turn in range(chunks + rounds):
        if turn < chunks:
            medium_and_states(turn)
            send_state(0, turn)
        for k in range(chunks):
            r = turn - k - 1
            if 0 <= r < rounds:
                take_state(r, k)
                if r + 1 < rounds:
                    send_state(r + 1, k)
        done = turn - rounds
        if 0 <= done < chunks:
            finish_chunk(done)

    sums = squares_out[...]
    for d in range(1, chan_n):
        squares_copy(d).start()
    for d in range(1, chan_n):
        squares_copy(d).wait_recv()
        sums = sums + squares_in[d - 1]
    width = chunks * CHUNK * chan_n
    inverse = lax.rsqrt(jnp.sum(sums, 1, keepdims=True) / width + 1e-06)

    for k in range(chunks):
        outb[k] = (acc[k] * inverse * ngain[:, cols(k)]).astype(bf16)
        pltpu.make_async_copy(outb.at[k], out_h.at[:, cols(k)], out_sem.at[k]).start()

    for k in range(chunks):
        pltpu.make_async_copy(outb.at[k], out_h.at[:, cols(k)], out_sem.at[k]).wait()

        @pl.when(pos < seq_n - 1)
        def _():
            halo_copy(k).wait_send()

        for r in range(rounds - 1):
            state_copy(r, k).wait_send()

        @pl.when(bits[rounds - 1] == 0)
        def _():
            state_copy(rounds - 1, k).wait_send()

    for d in range(1, chan_n):
        squares_copy(d).wait_send()


def per_device(
    seq_n, chan_n,
    hidden_in, query_mr, key_mr, value_mr, query_li, key_li,
    mr_filter, li_rate, li_residue, norm_gain,
):
    tokens, channels = hidden_in.shape
    groups = mr_filter.shape[1]
    modes = li_rate.shape[0]
    chunks = channels // CHUNK
    rounds = seq_n.bit_length() - 1
    slab = modes * SUBS
    assert seq_n == 1 << rounds and tokens == mr_filter.shape[0] == LANES
    big = pltpu.VMEM((chunks, tokens, CHUNK), bf16)
    dma = pltpu.SemaphoreType.DMA
    return pl.pallas_call(
        functools.partial(mixer_kernel, seq_n, chan_n, chunks, channels // groups),
        out_shape=jax.ShapeDtypeStruct((tokens, channels), bf16),
        in_specs=[pl.BlockSpec(memory_space=pl.ANY)] * 10,
        out_specs=pl.BlockSpec(memory_space=pl.ANY),
        scratch_shapes=[
            big, big, big, big, big, big,
            pltpu.VMEM(mr_filter.shape, bf16),
            pltpu.VMEM(li_rate.shape, f32),
            pltpu.VMEM(li_residue.shape, f32),
            pltpu.VMEM((1, channels), f32),
            big, big, big,
            pltpu.VMEM((groups, tokens), f32),
            pltpu.VMEM((channels // LANES, tokens, tokens * LANES * groups // channels), bf16),
            pltpu.VMEM((chunks, tokens, CHUNK), f32),
            pltpu.VMEM((channels // LANES * tokens, LANES), f32),
            pltpu.VMEM((chunks * slab, LANES), f32),
            pltpu.VMEM((chunks * slab, LANES), f32),
            pltpu.VMEM((chunks, slab, LANES), f32),
            pltpu.VMEM((chunks, slab, LANES), f32),
            pltpu.VMEM((rounds, chunks, slab, LANES), bf16),
            pltpu.VMEM((rounds, chunks, slab, LANES), bf16),
            pltpu.VMEM((tokens, LANES), f32),
            pltpu.VMEM((max(chan_n - 1, 1), tokens, LANES), f32),
            dma((6, chunks)),
            dma((4,)),
            dma((chunks,)),
            dma((chunks,)),
            dma((chunks,)),
            dma((rounds, chunks)),
            dma((rounds, chunks)),
            dma((max(chan_n - 1, 1),)),
            dma((max(chan_n - 1, 1),)),
        ],
        compiler_params=pltpu.CompilerParams(
            collective_id=0, has_side_effects=True, vmem_limit_bytes=63 * 1024 * 1024
        ),
        cost_estimate=pl.CostEstimate(
            flops=4 * tokens * tokens * channels * LANES * groups // channels,
            bytes_accessed=14 * tokens * channels,
            transcendentals=4 * modes * channels,
        ),
        name="hyena_mixers",
    )(
        hidden_in, query_mr, key_mr, value_mr, query_li, key_li,
        mr_filter, li_rate, li_residue, norm_gain.reshape(1, channels),
    )


def solution(mesh):
    seq_n, chan_n = mesh.shape["seq"], mesh.shape["chan"]
    rows = P("seq", "chan")
    by_channel = P(None, "chan")
    in_specs = (rows,) * 6 + (by_channel,) * 3 + (P("chan"),)
    return jax.shard_map(
        functools.partial(per_device, seq_n, chan_n),
        mesh=mesh, in_specs=in_specs, out_specs=rows, check_vma=False,
    )
```

```python
import functools

import jax
import jax.numpy as jnp
from jax import lax
from jax.experimental import pallas as pl
from jax.experimental.pallas import tpu as pltpu
from jax.sharding import PartitionSpec as P

LANES = 128
SUBS = 8
CHUNK = LANES * SUBS
f32 = jnp.float32
bf16 = jnp.bfloat16


def stages(seq_n):
    radices, spans = [], []
    span = 1
    while span < seq_n:
        radices.append(min(4, seq_n // span))
        spans.append(span)
        span *= radices[-1]
    return radices, spans


def mixer_kernel(
    seq_n, chan_n, chunks, group_width,
    hid_h, qmr_h, kmr_h, vmr_h, qli_h, kli_h, filt_h, rate_h, resid_h, gain_h,
    out_h,
    hid, qmr, kmr, vmr, qli, kli, filt, rate_in, resid_in, ngain,
    prod, halo, outb, taps, upper, acc, src, rate, mgain,
    prefix, total, state_out, state_in, squares_out, squares_in,
    in_sem, par_sem, out_sem, halo_send, halo_recv,
    st_send, st_recv, sq_send, sq_recv,
):
    pos = lax.axis_index("seq")
    lane_pos = lax.axis_index("chan")
    tokens = hid.shape[1]
    modes = rate_in.shape[0]
    slab = modes * SUBS
    radices, spans = stages(seq_n)
    rounds = len(radices)
    per_block = LANES // group_width
    nxt = lax.rem(pos + 1, seq_n)
    prv = lax.rem(pos + seq_n - 1, seq_n)

    def cols(k):
        return pl.ds(k * CHUNK, CHUNK)

    pairs = ((kmr_h, kmr), (vmr_h, vmr), (qmr_h, qmr), (kli_h, kli), (hid_h, hid), (qli_h, qli))

    def in_copy(a, k):
        return pltpu.make_async_copy(pairs[a][0].at[:, cols(k)], pairs[a][1].at[k], in_sem.at[a, k])

    par_copies = [
        pltpu.make_async_copy(h, v, par_sem.at[i])
        for i, (h, v) in enumerate(
            ((filt_h, filt), (rate_h, rate_in), (resid_h, resid_in), (gain_h, ngain))
        )
    ]
    for k in range(chunks):
        in_copy(0, k).start()
        in_copy(1, k).start()
    for c in par_copies:
        c.start()
    for a in range(2, 6):
        for k in range(chunks):
            in_copy(a, k).start()

    barrier = pltpu.get_barrier_semaphore()

    def greet(ids):
        pl.semaphore_signal(barrier, inc=1, device_id=ids, device_id_type=pl.DeviceIdType.MESH)

    greet({"seq": nxt})
    greet({"seq": prv})
    digits = [lax.rem(pos // m, q) for m, q in zip(spans, radices)]

    def member(r, e):
        return pos + spans[r] * (lax.rem(digits[r] + e, radices[r]) - digits[r])

    for r in range(rounds):
        for e in range(1, radices[r]):
            greet({"seq": member(r, e)})
    for d in range(1, chan_n):
        greet({"chan": lax.rem(lane_pos + d, chan_n)})

    def halo_copy(k):
        return pltpu.make_async_remote_copy(
            src_ref=prod.at[k], dst_ref=halo.at[k],
            send_sem=halo_send.at[k], recv_sem=halo_recv.at[k],
            device_id={"seq": nxt}, device_id_type=pl.DeviceIdType.MESH,
        )

    def state_copy(r, e, k):
        return pltpu.make_async_remote_copy(
            src_ref=state_out.at[r, k], dst_ref=state_in.at[r, e - 1, k],
            send_sem=st_send.at[r, e - 1, k], recv_sem=st_recv.at[r, e - 1, k],
            device_id={"seq": member(r, e)}, device_id_type=pl.DeviceIdType.MESH,
        )

    def squares_copy(d):
        return pltpu.make_async_remote_copy(
            src_ref=squares_out, dst_ref=squares_in.at[d - 1],
            send_sem=sq_send.at[d - 1], recv_sem=sq_recv.at[d - 1],
            device_id={"chan": lax.rem(lane_pos + d, chan_n)},
            device_id_type=pl.DeviceIdType.MESH,
        )

    @pl.when(pos == 0)
    def _():
        halo[...] = jnp.zeros_like(halo)

    for k in range(chunks):
        in_copy(0, k).wait()
        in_copy(1, k).wait()
        prod[k] = (kmr[k].astype(f32) * vmr[k].astype(f32)).astype(bf16)
        if k == 0:
            pl.semaphore_wait(barrier, 2 + sum(radices) - rounds + chan_n - 1)

        @pl.when(pos < seq_n - 1)
        def _():
            halo_copy(k).start()

    for c in par_copies:
        c.wait()

    tap_i = lax.broadcasted_iota(jnp.int32, (tokens, tokens), 0)
    pos_i = lax.broadcasted_iota(jnp.int32, (tokens, tokens), 1)
    wrap = jnp.where(lax.rem(tap_i + pos_i, tokens) == 0, 1.0, 0.0).astype(bf16)
    taps[...] = lax.dot_general(
        filt[...], wrap, (((0,), (0,)), ((), ())), preferred_element_type=f32
    )

    for k in range(chunks):
        for b in range(SUBS):
            lanes = pl.ds(k * CHUNK + b * LANES, LANES)
            r = rate_in[:, lanes]
            x = 2.0 * r
            series = x * (
                1.0 - x * (1 / 2) * (1.0 - x * (1 / 3) * (1.0 - x * (1 / 4) * (
                    1.0 - x * (1 / 5) * (1.0 - x * (1 / 6) * (1.0 - x * (1 / 7))))))
            )
            grown = jnp.where(x < 0.1, series, 1.0 - jnp.exp(-x))
            rows = pl.ds(k * slab + b, modes, stride=SUBS)
            rate[rows, :] = r
            mgain[rows, :] = resid_in[:, lanes] * jnp.sqrt(grown)

    def spread(x):
        lane = lax.broadcasted_iota(jnp.int32, x.shape, 1)
        wide = x.astype(f32)
        return jnp.concatenate(
            [
                jnp.where(lane // group_width == g, wide, 0.0).astype(bf16)
                for g in range(per_block)
            ],
            0,
        )

    row_i = lax.broadcasted_iota(jnp.int32, (tokens, LANES), 0)
    lane_i = lax.broadcasted_iota(jnp.int32, (tokens, LANES), 1)
    lower_mask = lane_i <= row_i

    for k in range(chunks):

        def local_block(b, carry):
            j = k * SUBS + b
            lanes = pl.ds(pl.multiple_of(b * LANES, LANES), LANES)
            rows = taps[pl.ds(pl.multiple_of(j * per_block, per_block), per_block), :]
            lows, ups = [], []
            for g in range(per_block):
                ring = pltpu.roll(
                    jnp.broadcast_to(rows[g : g + 1, :], (tokens, LANES)),
                    0, 1, stride=1, stride_axis=0,
                )
                lows.append(jnp.where(lower_mask, ring, 0.0).astype(bf16))
                ups.append(jnp.where(lower_mask, 0.0, ring).astype(bf16))
            upper[j] = jnp.concatenate(ups, 1)
            acc[k, :, lanes] = jnp.dot(
                jnp.concatenate(lows, 1), spread(prod[k, :, lanes]), preferred_element_type=f32
            )
            return carry

        lax.fori_loop(0, SUBS, local_block, 0)

    def chunk_rate(k):
        return rate[pl.ds(k * slab, slab), :]

    def chunk_mode(ref, k, n):
        return ref[pl.ds(k * slab + n * SUBS, SUBS), :]

    def medium_and_states(k):
        @pl.when(pos > 0)
        def _():
            halo_copy(k).wait_recv()

        for a in range(2, 5):
            in_copy(a, k).wait()

        def block(b, carry):
            j = k * SUBS + b
            lanes = pl.ds(pl.multiple_of(b * LANES, LANES), LANES)
            conv = acc[k, :, lanes] + jnp.dot(
                upper[j], spread(halo[k, :, lanes]), preferred_element_type=f32
            )
            out_mr = (qmr[k, :, lanes].astype(f32) * conv).astype(bf16).astype(f32)
            src[pl.ds(pl.multiple_of(j * tokens, tokens), tokens), :] = (
                kli[k, :, lanes].astype(f32) * out_mr
            )
            acc[k, :, lanes] = hid[k, :, lanes].astype(f32) + out_mr
            return carry

        lax.fori_loop(0, SUBS, block, 0)

        decay = [jnp.exp(-chunk_mode(rate, k, n)) for n in range(modes)]
        gain = [chunk_mode(mgain, k, n) for n in range(modes)]

        def step(t, states):
            at = pl.ds(k * SUBS * tokens + t, SUBS, stride=tokens)
            x = src[at, :]
            states = tuple(decay[n] * states[n] + x for n in range(modes))
            parts = [gain[n] * states[n] for n in range(modes)]
            while len(parts) > 1:
                parts = [a + b for a, b in zip(parts[::2], parts[1::2])]
            src[at, :] = parts[0]
            return states

        zero = jnp.zeros((SUBS, LANES), f32)
        states = lax.fori_loop(0, tokens, step, (zero,) * modes, unroll=16)
        for n in range(modes):
            total[k, pl.ds(n * SUBS, SUBS), :] = states[n]
        prefix[k] = jnp.zeros((slab, LANES), f32)

    def sends(r, e, act):
        if r < rounds - 1:
            act()
        else:
            pl.when(digits[r] + e < radices[r])(act)

    def takes(r, e, act):
        if r < rounds - 1:
            act()
        else:
            pl.when(digits[r] >= e)(act)

    def send_state(r, k):
        state_out[r, k] = total[k].astype(bf16)
        for e in range(1, radices[r]):
            sends(r, e, lambda: state_copy(r, e, k).start())

    def take_state(r, k):
        rates = chunk_rate(k)
        span, radix, digit = spans[r], radices[r], digits[r]
        inside = lax.rem(pos, span)

        def faded(steps, x):
            return jnp.exp(-rates * (tokens * steps).astype(f32)) * x

        if r < rounds - 1:
            total[k] = faded(span * (radix - 1 - digit), total[k])
        for e in range(1, radix):

            def take():
                state_copy(r, e, k).wait_recv()
                got = state_in[r, e - 1, k].astype(f32)
                sender = lax.rem(digit + radix - e, radix)
                earlier = sender < digit
                ahead = jnp.where(earlier, span * (digit - 1 - sender) + inside, 0)
                prefix[k] = prefix[k] + jnp.where(earlier, faded(ahead, got), 0.0)
                if r < rounds - 1:
                    total[k] = total[k] + faded(span * (radix - 1 - sender), got)

            takes(r, e, take)

    def finish_chunk(k):
        decay = [jnp.exp(-chunk_mode(rate, k, n)) for n in range(modes)]
        start = tuple(
            chunk_mode(mgain, k, n) * prefix[k, pl.ds(n * SUBS, SUBS), :] for n in range(modes)
        )

        def step(t, waves):
            at = pl.ds(k * SUBS * tokens + t, SUBS, stride=tokens)
            waves = tuple(decay[n] * waves[n] for n in range(modes))
            parts = list(waves)
            while len(parts) > 1:
                parts = [a + b for a, b in zip(parts[::2], parts[1::2])]
            src[at, :] = src[at, :] + parts[0]
            return waves

        lax.fori_loop(0, tokens, step, start, unroll=16)
        in_copy(5, k).wait()

        def block(b, carry):
            j = k * SUBS + b
            lanes = pl.ds(pl.multiple_of(b * LANES, LANES), LANES)
            conv = src[pl.ds(pl.multiple_of(j * tokens, tokens), tokens), :]
            combined = acc[k, :, lanes] + qli[k, :, lanes].astype(f32) * conv
            acc[k, :, lanes] = combined
            squares_out[...] += combined * combined
            return carry

        lax.fori_loop(0, SUBS, block, 0)

    squares_out[...] = jnp.zeros_like(squares_out)
    for turn in range(chunks + rounds):
        if turn < chunks:
            medium_and_states(turn)
            send_state(0, turn)
        for k in range(chunks):
            r = turn - k - 1
            if 0 <= r < rounds:
                take_state(r, k)
                if r + 1 < rounds:
                    send_state(r + 1, k)
        done = turn - rounds
        if 0 <= done < chunks:
            finish_chunk(done)

    sums = squares_out[...]
    for d in range(1, chan_n):
        squares_copy(d).start()
    for d in range(1, chan_n):
        squares_copy(d).wait_recv()
        sums = sums + squares_in[d - 1]
    width = chunks * CHUNK * chan_n
    inverse = lax.rsqrt(jnp.sum(sums, 1, keepdims=True) / width + 1e-06)

    for k in range(chunks):
        outb[k] = (acc[k] * inverse * ngain[:, cols(k)]).astype(bf16)
        pltpu.make_async_copy(outb.at[k], out_h.at[:, cols(k)], out_sem.at[k]).start()

    for k in range(chunks):
        pltpu.make_async_copy(outb.at[k], out_h.at[:, cols(k)], out_sem.at[k]).wait()

        @pl.when(pos < seq_n - 1)
        def _():
            halo_copy(k).wait_send()

        for r in range(rounds):
            for e in range(1, radices[r]):
                sends(r, e, lambda: state_copy(r, e, k).wait_send())

    for d in range(1, chan_n):
        squares_copy(d).wait_send()


def per_device(
    seq_n, chan_n,
    hidden_in, query_mr, key_mr, value_mr, query_li, key_li,
    mr_filter, li_rate, li_residue, norm_gain,
):
    tokens, channels = hidden_in.shape
    groups = mr_filter.shape[1]
    modes = li_rate.shape[0]
    chunks = channels // CHUNK
    radices, _ = stages(seq_n)
    rounds, most = len(radices), max(radices) - 1
    slab = modes * SUBS
    assert seq_n & (seq_n - 1) == 0 and tokens == mr_filter.shape[0] == LANES
    big = pltpu.VMEM((chunks, tokens, CHUNK), bf16)
    dma = pltpu.SemaphoreType.DMA
    return pl.pallas_call(
        functools.partial(mixer_kernel, seq_n, chan_n, chunks, channels // groups),
        out_shape=jax.ShapeDtypeStruct((tokens, channels), bf16),
        in_specs=[pl.BlockSpec(memory_space=pl.ANY)] * 10,
        out_specs=pl.BlockSpec(memory_space=pl.ANY),
        scratch_shapes=[
            big, big, big, big, big, big,
            pltpu.VMEM(mr_filter.shape, bf16),
            pltpu.VMEM(li_rate.shape, f32),
            pltpu.VMEM(li_residue.shape, f32),
            pltpu.VMEM((1, channels), f32),
            big, big, big,
            pltpu.VMEM((groups, tokens), f32),
            pltpu.VMEM((channels // LANES, tokens, tokens * LANES * groups // channels), bf16),
            pltpu.VMEM((chunks, tokens, CHUNK), f32),
            pltpu.VMEM((channels // LANES * tokens, LANES), f32),
            pltpu.VMEM((chunks * slab, LANES), f32),
            pltpu.VMEM((chunks * slab, LANES), f32),
            pltpu.VMEM((chunks, slab, LANES), f32),
            pltpu.VMEM((chunks, slab, LANES), f32),
            pltpu.VMEM((rounds, chunks, slab, LANES), bf16),
            pltpu.VMEM((rounds, most, chunks, slab, LANES), bf16),
            pltpu.VMEM((tokens, LANES), f32),
            pltpu.VMEM((max(chan_n - 1, 1), tokens, LANES), f32),
            dma((6, chunks)),
            dma((4,)),
            dma((chunks,)),
            dma((chunks,)),
            dma((chunks,)),
            dma((rounds, most, chunks)),
            dma((rounds, most, chunks)),
            dma((max(chan_n - 1, 1),)),
            dma((max(chan_n - 1, 1),)),
        ],
        compiler_params=pltpu.CompilerParams(
            collective_id=0, has_side_effects=True, vmem_limit_bytes=63 * 1024 * 1024
        ),
        cost_estimate=pl.CostEstimate(
            flops=4 * tokens * tokens * channels * LANES * groups // channels,
            bytes_accessed=14 * tokens * channels,
            transcendentals=4 * modes * channels,
        ),
        name="hyena_mixers",
    )(
        hidden_in, query_mr, key_mr, value_mr, query_li, key_li,
        mr_filter, li_rate, li_residue, norm_gain.reshape(1, channels),
    )


def solution(mesh):
    seq_n, chan_n = mesh.shape["seq"], mesh.shape["chan"]
    rows = P("seq", "chan")
    by_channel = P(None, "chan")
    in_specs = (rows,) * 6 + (by_channel,) * 3 + (P("chan"),)
    return jax.shard_map(
        functools.partial(per_device, seq_n, chan_n),
        mesh=mesh, in_specs=in_specs, out_specs=rows, check_vma=False,
    )
```

```python
import functools

import jax
import jax.numpy as jnp
from jax import lax
from jax.experimental import pallas as pl
from jax.experimental.pallas import tpu as pltpu
from jax.sharding import PartitionSpec as P

LANES = 128
SUBS = 8
CHUNK = LANES * SUBS
AHEAD = 2
f32 = jnp.float32
bf16 = jnp.bfloat16


def stages(seq_n):
    radices, spans = [], []
    span = 1
    while span < seq_n:
        radices.append(min(4, seq_n // span))
        spans.append(span)
        span *= radices[-1]
    return radices, spans


def mixer_kernel(
    seq_n, chan_n, chunks, group_width,
    hid_h, qmr_h, kmr_h, vmr_h, qli_h, kli_h, filt_h, rate_h, resid_h,
    out_h, inv_h,
    hid, qmr, kmr, vmr, qli, kli, filt, rate_in, resid_in,
    prod, halo, inv_b, taps, upper, acc, src, rate, mgain,
    prefix, total, state_out, state_in, squares_out, squares_in,
    in_sem, par_sem, out_sem, inv_sem, halo_send, halo_recv,
    st_send, st_recv, sq_send, sq_recv,
):
    pos = lax.axis_index("seq")
    lane_pos = lax.axis_index("chan")
    tokens = hid.shape[1]
    modes = rate_in.shape[0]
    slab = modes * SUBS
    radices, spans = stages(seq_n)
    rounds = len(radices)
    per_block = LANES // group_width
    nxt = lax.rem(pos + 1, seq_n)
    prv = lax.rem(pos + seq_n - 1, seq_n)

    def cols(k):
        return pl.ds(k * CHUNK, CHUNK)

    pairs = ((kmr_h, kmr), (vmr_h, vmr), (qmr_h, qmr), (kli_h, kli), (hid_h, hid), (qli_h, qli))

    def in_copy(a, k):
        return pltpu.make_async_copy(pairs[a][0].at[:, cols(k)], pairs[a][1].at[k], in_sem.at[a, k])

    par_copies = [
        pltpu.make_async_copy(h, v, par_sem.at[i])
        for i, (h, v) in enumerate(
            ((filt_h, filt), (rate_h, rate_in), (resid_h, resid_in))
        )
    ]
    for k in range(chunks):
        in_copy(0, k).start()
        in_copy(1, k).start()
    for c in par_copies:
        c.start()
    for a in range(2, 6):
        for k in range(chunks):
            in_copy(a, k).start()

    barrier = pltpu.get_barrier_semaphore()

    def greet(ids):
        pl.semaphore_signal(barrier, inc=1, device_id=ids, device_id_type=pl.DeviceIdType.MESH)

    greet({"seq": nxt})
    greet({"seq": prv})
    digits = [lax.rem(pos // m, q) for m, q in zip(spans, radices)]

    def member(r, e):
        return pos + spans[r] * (lax.rem(digits[r] + e, radices[r]) - digits[r])

    for r in range(rounds):
        for e in range(1, radices[r]):
            greet({"seq": member(r, e)})
    for d in range(1, chan_n):
        greet({"chan": lax.rem(lane_pos + d, chan_n)})

    def halo_copy(k):
        return pltpu.make_async_remote_copy(
            src_ref=prod.at[k], dst_ref=halo.at[k],
            send_sem=halo_send.at[k], recv_sem=halo_recv.at[k],
            device_id={"seq": nxt}, device_id_type=pl.DeviceIdType.MESH,
        )

    def state_copy(r, e, k):
        return pltpu.make_async_remote_copy(
            src_ref=state_out.at[r, k], dst_ref=state_in.at[r, e - 1, k],
            send_sem=st_send.at[r, e - 1, k], recv_sem=st_recv.at[r, e - 1, k],
            device_id={"seq": member(r, e)}, device_id_type=pl.DeviceIdType.MESH,
        )

    def squares_copy(d):
        return pltpu.make_async_remote_copy(
            src_ref=squares_out, dst_ref=squares_in.at[d - 1],
            send_sem=sq_send.at[d - 1], recv_sem=sq_recv.at[d - 1],
            device_id={"chan": lax.rem(lane_pos + d, chan_n)},
            device_id_type=pl.DeviceIdType.MESH,
        )

    def start_halo(k):
        pl.when(pos < seq_n - 1)(lambda: halo_copy(k).start())

    def halo_sent(k):
        pl.when(pos < seq_n - 1)(lambda: halo_copy(k).wait_send())

    @pl.when(pos == 0)
    def _():
        halo[...] = jnp.zeros_like(halo)

    for k in range(chunks):
        in_copy(0, k).wait()
        in_copy(1, k).wait()
        prod[k] = (kmr[k].astype(f32) * vmr[k].astype(f32)).astype(bf16)
        if k == 0:
            pl.semaphore_wait(barrier, 2 + sum(radices) - rounds + chan_n - 1)

        if k < AHEAD:
            start_halo(k)

    for c in par_copies:
        c.wait()

    tap_i = lax.broadcasted_iota(jnp.int32, (tokens, tokens), 0)
    pos_i = lax.broadcasted_iota(jnp.int32, (tokens, tokens), 1)
    wrap = jnp.where(lax.rem(tap_i + pos_i, tokens) == 0, 1.0, 0.0).astype(bf16)
    taps[...] = lax.dot_general(
        filt[...], wrap, (((0,), (0,)), ((), ())), preferred_element_type=f32
    )

    for k in range(chunks):
        for b in range(SUBS):
            lanes = pl.ds(k * CHUNK + b * LANES, LANES)
            r = rate_in[:, lanes]
            x = 2.0 * r
            series = x * (
                1.0 - x * (1 / 2) * (1.0 - x * (1 / 3) * (1.0 - x * (1 / 4) * (
                    1.0 - x * (1 / 5) * (1.0 - x * (1 / 6) * (1.0 - x * (1 / 7))))))
            )
            grown = jnp.where(x < 0.1, series, 1.0 - jnp.exp(-x))
            rows = pl.ds(k * slab + b, modes, stride=SUBS)
            rate[rows, :] = r
            mgain[rows, :] = resid_in[:, lanes] * jnp.sqrt(grown)

    def spread(x):
        lane = lax.broadcasted_iota(jnp.int32, x.shape, 1)
        wide = x.astype(f32)
        return jnp.concatenate(
            [
                jnp.where(lane // group_width == g, wide, 0.0).astype(bf16)
                for g in range(per_block)
            ],
            0,
        )

    row_i = lax.broadcasted_iota(jnp.int32, (tokens, LANES), 0)
    lane_i = lax.broadcasted_iota(jnp.int32, (tokens, LANES), 1)
    lower_mask = lane_i <= row_i

    for k in range(chunks):

        def local_block(b, carry):
            j = k * SUBS + b
            lanes = pl.ds(pl.multiple_of(b * LANES, LANES), LANES)
            rows = taps[pl.ds(pl.multiple_of(j * per_block, per_block), per_block), :]
            lows, ups = [], []
            for g in range(per_block):
                ring = pltpu.roll(
                    jnp.broadcast_to(rows[g : g + 1, :], (tokens, LANES)),
                    0, 1, stride=1, stride_axis=0,
                )
                lows.append(jnp.where(lower_mask, ring, 0.0).astype(bf16))
                ups.append(jnp.where(lower_mask, 0.0, ring).astype(bf16))
            upper[j] = jnp.concatenate(ups, 1)
            acc[k, :, lanes] = jnp.dot(
                jnp.concatenate(lows, 1), spread(prod[k, :, lanes]), preferred_element_type=f32
            )
            return carry

        lax.fori_loop(0, SUBS, local_block, 0)

    def chunk_rate(k):
        return rate[pl.ds(k * slab, slab), :]

    def chunk_mode(ref, k, n):
        return ref[pl.ds(k * slab + n * SUBS, SUBS), :]

    def medium_and_states(k):
        @pl.when(pos > 0)
        def _():
            halo_copy(k).wait_recv()

        for a in range(2, 5):
            in_copy(a, k).wait()

        def block(b, carry):
            j = k * SUBS + b
            lanes = pl.ds(pl.multiple_of(b * LANES, LANES), LANES)
            conv = acc[k, :, lanes] + jnp.dot(
                upper[j], spread(halo[k, :, lanes]), preferred_element_type=f32
            )
            out_mr = (qmr[k, :, lanes].astype(f32) * conv).astype(bf16).astype(f32)
            src[pl.ds(pl.multiple_of(j * tokens, tokens), tokens), :] = (
                kli[k, :, lanes].astype(f32) * out_mr
            )
            acc[k, :, lanes] = hid[k, :, lanes].astype(f32) + out_mr
            return carry

        lax.fori_loop(0, SUBS, block, 0)

        decay = [jnp.exp(-chunk_mode(rate, k, n)) for n in range(modes)]
        gain = [chunk_mode(mgain, k, n) for n in range(modes)]

        def step(t, states):
            at = pl.ds(k * SUBS * tokens + t, SUBS, stride=tokens)
            x = src[at, :]
            states = tuple(decay[n] * states[n] + x for n in range(modes))
            parts = [gain[n] * states[n] for n in range(modes)]
            while len(parts) > 1:
                parts = [a + b for a, b in zip(parts[::2], parts[1::2])]
            src[at, :] = parts[0]
            return states

        zero = jnp.zeros((SUBS, LANES), f32)
        states = lax.fori_loop(0, tokens, step, (zero,) * modes, unroll=16)
        for n in range(modes):
            total[k, pl.ds(n * SUBS, SUBS), :] = states[n]
        prefix[k] = jnp.zeros((slab, LANES), f32)

    def sends(r, e, act):
        if r < rounds - 1:
            act()
        else:
            pl.when(digits[r] + e < radices[r])(act)

    def takes(r, e, act):
        if r < rounds - 1:
            act()
        else:
            pl.when(digits[r] >= e)(act)

    def send_state(r, k):
        state_out[r, k] = total[k].astype(bf16)
        for e in range(1, radices[r]):
            sends(r, e, lambda: state_copy(r, e, k).start())

    def take_state(r, k):
        rates = chunk_rate(k)
        span, radix, digit = spans[r], radices[r], digits[r]
        inside = lax.rem(pos, span)

        def faded(steps, x):
            return jnp.exp(-rates * (tokens * steps).astype(f32)) * x

        if r < rounds - 1:
            total[k] = faded(span * (radix - 1 - digit), total[k])
        for e in range(1, radix):

            def take():
                state_copy(r, e, k).wait_recv()
                got = state_in[r, e - 1, k].astype(f32)
                sender = lax.rem(digit + radix - e, radix)
                earlier = sender < digit
                ahead = jnp.where(earlier, span * (digit - 1 - sender) + inside, 0)
                prefix[k] = prefix[k] + jnp.where(earlier, faded(ahead, got), 0.0)
                if r < rounds - 1:
                    total[k] = total[k] + faded(span * (radix - 1 - sender), got)

            takes(r, e, take)

    def out_copy(k):
        return pltpu.make_async_copy(acc.at[k], out_h.at[:, cols(k)], out_sem.at[k])

    def finish_chunk(k):
        decay = [jnp.exp(-chunk_mode(rate, k, n)) for n in range(modes)]
        start = tuple(
            chunk_mode(mgain, k, n) * prefix[k, pl.ds(n * SUBS, SUBS), :] for n in range(modes)
        )

        def step(t, waves):
            at = pl.ds(k * SUBS * tokens + t, SUBS, stride=tokens)
            waves = tuple(decay[n] * waves[n] for n in range(modes))
            parts = list(waves)
            while len(parts) > 1:
                parts = [a + b for a, b in zip(parts[::2], parts[1::2])]
            src[at, :] = src[at, :] + parts[0]
            return waves

        lax.fori_loop(0, tokens, step, start, unroll=16)
        in_copy(5, k).wait()

        def block(b, carry):
            j = k * SUBS + b
            lanes = pl.ds(pl.multiple_of(b * LANES, LANES), LANES)
            conv = src[pl.ds(pl.multiple_of(j * tokens, tokens), tokens), :]
            combined = acc[k, :, lanes] + qli[k, :, lanes].astype(f32) * conv
            acc[k, :, lanes] = combined
            squares_out[...] += combined * combined
            return carry

        lax.fori_loop(0, SUBS, block, 0)
        out_copy(k).start()

    squares_out[...] = jnp.zeros_like(squares_out)
    for turn in range(chunks + rounds):
        if turn < chunks:
            halo_sent(turn)
            if turn + AHEAD < chunks:
                start_halo(turn + AHEAD)
            medium_and_states(turn)
            send_state(0, turn)
        for k in range(chunks):
            r = turn - k - 1
            if 0 <= r < rounds:
                take_state(r, k)
                if r + 1 < rounds:
                    send_state(r + 1, k)
        done = turn - rounds
        if 0 <= done < chunks:
            finish_chunk(done)

    sums = squares_out[...]
    for d in range(1, chan_n):
        squares_copy(d).start()
    for d in range(1, chan_n):
        squares_copy(d).wait_recv()
        sums = sums + squares_in[d - 1]
    width = chunks * CHUNK * chan_n
    inverse = lax.rsqrt(jnp.sum(sums, 1, keepdims=True) / width + 1e-06)
    inv_b[...] = jnp.broadcast_to(inverse, inv_b.shape)
    inv_copy = pltpu.make_async_copy(inv_b, inv_h, inv_sem)
    inv_copy.start()
    inv_copy.wait()

    for k in range(chunks):
        out_copy(k).wait()
        for r in range(rounds):
            for e in range(1, radices[r]):
                sends(r, e, lambda: state_copy(r, e, k).wait_send())

    for d in range(1, chan_n):
        squares_copy(d).wait_send()


def norm_kernel(combined, inverse, gain, out):
    out[...] = (combined[...] * inverse[:, :1] * gain[...]).astype(bf16)


def per_device(
    seq_n, chan_n,
    hidden_in, query_mr, key_mr, value_mr, query_li, key_li,
    mr_filter, li_rate, li_residue, norm_gain,
):
    tokens, channels = hidden_in.shape
    groups = mr_filter.shape[1]
    modes = li_rate.shape[0]
    chunks = channels // CHUNK
    radices, _ = stages(seq_n)
    rounds, most = len(radices), max(radices) - 1
    slab = modes * SUBS
    assert seq_n & (seq_n - 1) == 0 and tokens == mr_filter.shape[0] == LANES
    big = pltpu.VMEM((chunks, tokens, CHUNK), bf16)
    dma = pltpu.SemaphoreType.DMA
    combined, inverse = pl.pallas_call(
        functools.partial(mixer_kernel, seq_n, chan_n, chunks, channels // groups),
        out_shape=(
            jax.ShapeDtypeStruct((tokens, channels), f32),
            jax.ShapeDtypeStruct((tokens, LANES), f32),
        ),
        in_specs=[pl.BlockSpec(memory_space=pl.ANY)] * 9,
        out_specs=(pl.BlockSpec(memory_space=pl.ANY),) * 2,
        scratch_shapes=[
            big, big, big, big, big, big,
            pltpu.VMEM(mr_filter.shape, bf16),
            pltpu.VMEM(li_rate.shape, f32),
            pltpu.VMEM(li_residue.shape, f32),
            big, big,
            pltpu.VMEM((tokens, LANES), f32),
            pltpu.VMEM((groups, tokens), f32),
            pltpu.VMEM((channels // LANES, tokens, tokens * LANES * groups // channels), bf16),
            pltpu.VMEM((chunks, tokens, CHUNK), f32),
            pltpu.VMEM((channels // LANES * tokens, LANES), f32),
            pltpu.VMEM((chunks * slab, LANES), f32),
            pltpu.VMEM((chunks * slab, LANES), f32),
            pltpu.VMEM((chunks, slab, LANES), f32),
            pltpu.VMEM((chunks, slab, LANES), f32),
            pltpu.VMEM((rounds, chunks, slab, LANES), bf16),
            pltpu.VMEM((rounds, most, chunks, slab, LANES), bf16),
            pltpu.VMEM((tokens, LANES), f32),
            pltpu.VMEM((max(chan_n - 1, 1), tokens, LANES), f32),
            dma((6, chunks)),
            dma((3,)),
            dma((chunks,)),
            dma,
            dma((chunks,)),
            dma((chunks,)),
            dma((rounds, most, chunks)),
            dma((rounds, most, chunks)),
            dma((max(chan_n - 1, 1),)),
            dma((max(chan_n - 1, 1),)),
        ],
        compiler_params=pltpu.CompilerParams(
            collective_id=0, has_side_effects=True, vmem_limit_bytes=63 * 1024 * 1024
        ),
        cost_estimate=pl.CostEstimate(
            flops=4 * tokens * tokens * channels * LANES * groups // channels,
            bytes_accessed=14 * tokens * channels,
            transcendentals=4 * modes * channels,
        ),
        name="hyena_mixers",
    )(
        hidden_in, query_mr, key_mr, value_mr, query_li, key_li,
        mr_filter, li_rate, li_residue,
    )
    block = pl.BlockSpec((tokens, CHUNK), lambda i: (0, i))
    return pl.pallas_call(
        norm_kernel,
        grid=(chunks,),
        out_shape=jax.ShapeDtypeStruct((tokens, channels), bf16),
        in_specs=[
            block,
            pl.BlockSpec((tokens, LANES), lambda i: (0, 0)),
            pl.BlockSpec((1, CHUNK), lambda i: (0, i)),
        ],
        out_specs=block,
        name="rms_scale",
    )(combined, inverse, norm_gain.reshape(1, channels))


def solution(mesh):
    seq_n, chan_n = mesh.shape["seq"], mesh.shape["chan"]
    rows = P("seq", "chan")
    by_channel = P(None, "chan")
    in_specs = (rows,) * 6 + (by_channel,) * 3 + (P("chan"),)
    return jax.shard_map(
        functools.partial(per_device, seq_n, chan_n),
        mesh=mesh, in_specs=in_specs, out_specs=rows, check_vma=False,
    )
```

```python
import functools

import jax
import jax.numpy as jnp
from jax import lax
from jax.experimental import pallas as pl
from jax.experimental.pallas import tpu as pltpu
from jax.sharding import PartitionSpec as P

LANES = 128
SUBS = 8
CHUNK = LANES * SUBS
AHEAD = 2
PAIR = 16
f32 = jnp.float32
bf16 = jnp.bfloat16


def stages(seq_n):
    radices, spans = [], []
    span = 1
    while span < seq_n:
        radices.append(min(4, seq_n // span))
        spans.append(span)
        span *= radices[-1]
    return radices, spans


def mixer_kernel(
    seq_n, chan_n, chunks, group_width,
    hid_h, qmr_h, kmr_h, vmr_h, qli_h, kli_h, filt_h, rate_h, resid_h, gain_h,
    out_h,
    hid, qmr, kmr, vmr, qli, kli, filt, rate_in, resid_in, ngain,
    spill, halo, outb, taps, acc, src, rate, mgain,
    prefix, total, state_out, state_in, squares_out, squares_in,
    in_sem, par_sem, out_sem, halo_send, halo_recv,
    st_send, st_recv, sq_send, sq_recv,
):
    pos = lax.axis_index("seq")
    lane_pos = lax.axis_index("chan")
    tokens = hid.shape[1]
    modes = rate_in.shape[0]
    slab = modes * SUBS
    pitch = tokens + SUBS
    radices, spans = stages(seq_n)
    rounds = len(radices)
    per_block = LANES // group_width
    nxt = lax.rem(pos + 1, seq_n)
    prv = lax.rem(pos + seq_n - 1, seq_n)

    def cols(k):
        return pl.ds(k * CHUNK, CHUNK)

    pairs = ((kmr_h, kmr), (vmr_h, vmr), (qmr_h, qmr), (kli_h, kli), (hid_h, hid), (qli_h, qli))

    def in_copy(a, k):
        return pltpu.make_async_copy(pairs[a][0].at[:, cols(k)], pairs[a][1].at[k], in_sem.at[a, k])

    par_copies = [
        pltpu.make_async_copy(h, v, par_sem.at[i])
        for i, (h, v) in enumerate(
            ((filt_h, filt), (rate_h, rate_in), (resid_h, resid_in), (gain_h, ngain))
        )
    ]
    par_copies[0].start()
    for k in range(chunks):
        in_copy(0, k).start()
        in_copy(1, k).start()
    for c in par_copies[1:]:
        c.start()
    for a in range(2, 6):
        for k in range(chunks):
            in_copy(a, k).start()

    barrier = pltpu.get_barrier_semaphore()

    def greet(ids):
        pl.semaphore_signal(barrier, inc=1, device_id=ids, device_id_type=pl.DeviceIdType.MESH)

    greet({"seq": nxt})
    greet({"seq": prv})
    digits = [lax.rem(pos // m, q) for m, q in zip(spans, radices)]

    def member(r, e):
        return pos + spans[r] * (lax.rem(digits[r] + e, radices[r]) - digits[r])

    for r in range(rounds):
        for e in range(1, radices[r]):
            greet({"seq": member(r, e)})
    for d in range(1, chan_n):
        greet({"chan": lax.rem(lane_pos + d, chan_n)})

    def halo_copy(k):
        return pltpu.make_async_remote_copy(
            src_ref=spill.at[k], dst_ref=halo.at[k],
            send_sem=halo_send.at[k], recv_sem=halo_recv.at[k],
            device_id={"seq": nxt}, device_id_type=pl.DeviceIdType.MESH,
        )

    def state_copy(r, e, k):
        return pltpu.make_async_remote_copy(
            src_ref=state_out.at[r, k], dst_ref=state_in.at[r, e - 1, k],
            send_sem=st_send.at[r, e - 1, k], recv_sem=st_recv.at[r, e - 1, k],
            device_id={"seq": member(r, e)}, device_id_type=pl.DeviceIdType.MESH,
        )

    def squares_copy(d):
        return pltpu.make_async_remote_copy(
            src_ref=squares_out, dst_ref=squares_in.at[d - 1],
            send_sem=sq_send.at[d - 1], recv_sem=sq_recv.at[d - 1],
            device_id={"chan": lax.rem(lane_pos + d, chan_n)},
            device_id_type=pl.DeviceIdType.MESH,
        )

    def start_halo(k):
        pl.when(pos < seq_n - 1)(lambda: halo_copy(k).start())

    def halo_sent(k):
        pl.when(pos < seq_n - 1)(lambda: halo_copy(k).wait_send())

    @pl.when(pos == 0)
    def _():
        halo[...] = jnp.zeros_like(halo)

    for c in par_copies:
        c.wait()

    tap_i = lax.broadcasted_iota(jnp.int32, (tokens, tokens), 0)
    pos_i = lax.broadcasted_iota(jnp.int32, (tokens, tokens), 1)
    wrap = jnp.where(lax.rem(tap_i + pos_i, tokens) == 0, 1.0, 0.0).astype(bf16)
    taps[...] = lax.dot_general(
        filt[...], wrap, (((0,), (0,)), ((), ())), preferred_element_type=f32
    )

    for k in range(chunks):
        for b in range(SUBS):
            lanes = pl.ds(k * CHUNK + b * LANES, LANES)
            r = rate_in[:, lanes]
            x = 2.0 * r
            series = x * (
                1.0 - x * (1 / 2) * (1.0 - x * (1 / 3) * (1.0 - x * (1 / 4) * (
                    1.0 - x * (1 / 5) * (1.0 - x * (1 / 6) * (1.0 - x * (1 / 7))))))
            )
            grown = jnp.where(x < 0.1, series, 1.0 - jnp.exp(-x))
            rows = pl.ds(k * slab + b, modes, stride=SUBS)
            rate[rows, :] = r
            mgain[rows, :] = resid_in[:, lanes] * jnp.sqrt(grown)

    group_of_lane = lax.broadcasted_iota(jnp.int32, (tokens, LANES), 1) // group_width
    member_lanes = [jnp.where(group_of_lane == g, 1.0, 0.0).astype(bf16) for g in range(per_block)]
    lags = lax.broadcasted_iota(jnp.int32, (tokens, LANES), 0) - lax.broadcasted_iota(
        jnp.int32, (tokens, LANES), 1
    )
    lower = jnp.where(lags >= 0, 1.0, 0.0).astype(bf16)
    higher = jnp.where(lags >= 0, 0.0, 1.0).astype(bf16)

    for k in range(chunks):
        in_copy(0, k).wait()
        in_copy(1, k).wait()

        def local_block(b, carry):
            j = k * SUBS + b
            lanes = pl.ds(pl.multiple_of(b * LANES, LANES), LANES)
            product = (kmr[k, :, lanes].astype(f32) * vmr[k, :, lanes].astype(f32)).astype(bf16)
            rows = taps[pl.ds(pl.multiple_of(j * per_block, per_block), per_block), :]
            own, over = [], []
            for g in range(per_block):
                first = pltpu.roll(
                    jnp.broadcast_to(rows[g : g + 1, :], (PAIR, LANES)),
                    0, 1, stride=1, stride_axis=0,
                ).astype(bf16)
                ring = jnp.concatenate(
                    [first] + [pltpu.roll(first, i, 1) for i in range(PAIR, tokens, PAIR)], 0
                )
                own.append(ring * lower)
                over.append(ring * higher)
            result = jnp.dot(
                jnp.concatenate([jnp.concatenate(own, 1), jnp.concatenate(over, 1)], 0),
                jnp.concatenate([product * m for m in member_lanes], 0),
                preferred_element_type=f32,
            )
            acc[k, :, lanes] = result[:tokens]
            spill[k, :, lanes] = result[tokens:].astype(bf16)
            return carry

        lax.fori_loop(0, SUBS, local_block, 0)
        if k == 0:
            pl.semaphore_wait(barrier, 2 + sum(radices) - rounds + chan_n - 1)
        if k < AHEAD:
            start_halo(k)

    def chunk_rate(k):
        return rate[pl.ds(k * slab, slab), :]

    def chunk_mode(ref, k, n):
        return ref[pl.ds(k * slab + n * SUBS, SUBS), :]

    def medium_and_states(k):
        @pl.when(pos > 0)
        def _():
            halo_copy(k).wait_recv()

        for a in range(2, 5):
            in_copy(a, k).wait()

        def block(b, carry):
            j = k * SUBS + b
            lanes = pl.ds(pl.multiple_of(b * LANES, LANES), LANES)
            conv = acc[k, :, lanes] + halo[k, :, lanes].astype(f32)
            out_mr = (qmr[k, :, lanes].astype(f32) * conv).astype(bf16).astype(f32)
            src[pl.ds(pl.multiple_of(j * pitch, SUBS), tokens), :] = (
                kli[k, :, lanes].astype(f32) * out_mr
            )
            acc[k, :, lanes] = hid[k, :, lanes].astype(f32) + out_mr
            return carry

        lax.fori_loop(0, SUBS, block, 0)

        decay = [jnp.exp(-chunk_mode(rate, k, n)) for n in range(modes)]
        gain = [chunk_mode(mgain, k, n) for n in range(modes)]

        def step(t, states):
            at = pl.ds(k * SUBS * pitch + t, SUBS, stride=pitch)
            x = src[at, :]
            states = tuple(decay[n] * states[n] + x for n in range(modes))
            parts = [gain[n] * states[n] for n in range(modes)]
            while len(parts) > 1:
                parts = [a + b for a, b in zip(parts[::2], parts[1::2])]
            src[at, :] = parts[0]
            return states

        zero = jnp.zeros((SUBS, LANES), f32)
        states = lax.fori_loop(0, tokens, step, (zero,) * modes, unroll=16)
        for n in range(modes):
            total[k, pl.ds(n * SUBS, SUBS), :] = states[n]
        prefix[k] = jnp.zeros((slab, LANES), f32)

    def sends(r, e, act):
        if r < rounds - 1:
            act()
        else:
            pl.when(digits[r] + e < radices[r])(act)

    def takes(r, e, act):
        if r < rounds - 1:
            act()
        else:
            pl.when(digits[r] >= e)(act)

    def send_state(r, k):
        state_out[r, k] = total[k].astype(bf16)
        for e in range(1, radices[r]):
            sends(r, e, lambda: state_copy(r, e, k).start())

    def take_state(r, k):
        rates = chunk_rate(k)
        span, radix, digit = spans[r], radices[r], digits[r]
        inside = lax.rem(pos, span)

        def faded(steps, x):
            return jnp.exp(-rates * (tokens * steps).astype(f32)) * x

        if r < rounds - 1:
            total[k] = faded(span * (radix - 1 - digit), total[k])
        for e in range(1, radix):

            def take():
                state_copy(r, e, k).wait_recv()
                got = state_in[r, e - 1, k].astype(f32)
                sender = lax.rem(digit + radix - e, radix)
                earlier = sender < digit
                ahead = jnp.where(earlier, span * (digit - 1 - sender) + inside, 0)
                prefix[k] = prefix[k] + jnp.where(earlier, faded(ahead, got), 0.0)
                if r < rounds - 1:
                    total[k] = total[k] + faded(span * (radix - 1 - sender), got)

            takes(r, e, take)

    def finish_chunk(k):
        decay = [jnp.exp(-chunk_mode(rate, k, n)) for n in range(modes)]
        start = tuple(
            chunk_mode(mgain, k, n) * prefix[k, pl.ds(n * SUBS, SUBS), :] for n in range(modes)
        )

        def step(t, waves):
            at = pl.ds(k * SUBS * pitch + t, SUBS, stride=pitch)
            waves = tuple(decay[n] * waves[n] for n in range(modes))
            parts = list(waves)
            while len(parts) > 1:
                parts = [a + b for a, b in zip(parts[::2], parts[1::2])]
            src[at, :] = src[at, :] + parts[0]
            return waves

        lax.fori_loop(0, tokens, step, start, unroll=16)
        in_copy(5, k).wait()

        def block(b, carry):
            j = k * SUBS + b
            lanes = pl.ds(pl.multiple_of(b * LANES, LANES), LANES)
            conv = src[pl.ds(pl.multiple_of(j * pitch, SUBS), tokens), :]
            combined = acc[k, :, lanes] + qli[k, :, lanes].astype(f32) * conv
            acc[k, :, lanes] = combined
            squares_out[...] += combined * combined
            return carry

        lax.fori_loop(0, SUBS, block, 0)

    squares_out[...] = jnp.zeros_like(squares_out)
    for turn in range(chunks + rounds):
        if turn < chunks:
            halo_sent(turn)
            if turn + AHEAD < chunks:
                start_halo(turn + AHEAD)
            medium_and_states(turn)
            send_state(0, turn)
        for k in range(chunks):
            r = turn - k - 1
            if 0 <= r < rounds:
                take_state(r, k)
                if r + 1 < rounds:
                    send_state(r + 1, k)
        done = turn - rounds
        if 0 <= done < chunks:
            finish_chunk(done)

    sums = squares_out[...]
    for d in range(1, chan_n):
        squares_copy(d).start()
    for d in range(1, chan_n):
        squares_copy(d).wait_recv()
        sums = sums + squares_in[d - 1]
    width = chunks * CHUNK * chan_n
    inverse = lax.rsqrt(jnp.sum(sums, 1, keepdims=True) / width + 1e-06)

    for k in range(chunks):
        outb[k] = (acc[k] * inverse * ngain[:, cols(k)]).astype(bf16)
        pltpu.make_async_copy(outb.at[k], out_h.at[:, cols(k)], out_sem.at[k]).start()

    for k in range(chunks):
        pltpu.make_async_copy(outb.at[k], out_h.at[:, cols(k)], out_sem.at[k]).wait()

        for r in range(rounds):
            for e in range(1, radices[r]):
                sends(r, e, lambda: state_copy(r, e, k).wait_send())

    for d in range(1, chan_n):
        squares_copy(d).wait_send()


def per_device(
    seq_n, chan_n,
    hidden_in, query_mr, key_mr, value_mr, query_li, key_li,
    mr_filter, li_rate, li_residue, norm_gain,
):
    tokens, channels = hidden_in.shape
    groups = mr_filter.shape[1]
    modes = li_rate.shape[0]
    chunks = channels // CHUNK
    radices, _ = stages(seq_n)
    rounds, most = len(radices), max(radices) - 1
    slab = modes * SUBS
    assert seq_n & (seq_n - 1) == 0 and tokens == mr_filter.shape[0] == LANES
    big = pltpu.VMEM((chunks, tokens, CHUNK), bf16)
    dma = pltpu.SemaphoreType.DMA
    return pl.pallas_call(
        functools.partial(mixer_kernel, seq_n, chan_n, chunks, channels // groups),
        out_shape=jax.ShapeDtypeStruct((tokens, channels), bf16),
        in_specs=[pl.BlockSpec(memory_space=pl.ANY)] * 10,
        out_specs=pl.BlockSpec(memory_space=pl.ANY),
        scratch_shapes=[
            big, big, big, big, big, big,
            pltpu.VMEM(mr_filter.shape, bf16),
            pltpu.VMEM(li_rate.shape, f32),
            pltpu.VMEM(li_residue.shape, f32),
            pltpu.VMEM((1, channels), f32),
            big, big, big,
            pltpu.VMEM((groups, tokens), f32),
            pltpu.VMEM((chunks, tokens, CHUNK), f32),
            pltpu.VMEM((channels // LANES * (tokens + SUBS), LANES), f32),
            pltpu.VMEM((chunks * slab, LANES), f32),
            pltpu.VMEM((chunks * slab, LANES), f32),
            pltpu.VMEM((chunks, slab, LANES), f32),
            pltpu.VMEM((chunks, slab, LANES), f32),
            pltpu.VMEM((rounds, chunks, slab, LANES), bf16),
            pltpu.VMEM((rounds, most, chunks, slab, LANES), bf16),
            pltpu.VMEM((tokens, LANES), f32),
            pltpu.VMEM((max(chan_n - 1, 1), tokens, LANES), f32),
            dma((6, chunks)),
            dma((4,)),
            dma((chunks,)),
            dma((chunks,)),
            dma((chunks,)),
            dma((rounds, most, chunks)),
            dma((rounds, most, chunks)),
            dma((max(chan_n - 1, 1),)),
            dma((max(chan_n - 1, 1),)),
        ],
        compiler_params=pltpu.CompilerParams(
            collective_id=0, has_side_effects=True, vmem_limit_bytes=63 * 1024 * 1024
        ),
        cost_estimate=pl.CostEstimate(
            flops=4 * tokens * tokens * channels * LANES * groups // channels,
            bytes_accessed=14 * tokens * channels,
            transcendentals=4 * modes * channels,
        ),
        name="hyena_mixers",
    )(
        hidden_in, query_mr, key_mr, value_mr, query_li, key_li,
        mr_filter, li_rate, li_residue, norm_gain.reshape(1, channels),
    )


def solution(mesh):
    seq_n, chan_n = mesh.shape["seq"], mesh.shape["chan"]
    rows = P("seq", "chan")
    by_channel = P(None, "chan")
    in_specs = (rows,) * 6 + (by_channel,) * 3 + (P("chan"),)
    return jax.shard_map(
        functools.partial(per_device, seq_n, chan_n),
        mesh=mesh, in_specs=in_specs, out_specs=rows, check_vma=False,
    )
```

```python
import functools

import jax
import jax.numpy as jnp
from jax import lax
from jax.experimental import pallas as pl
from jax.experimental.pallas import tpu as pltpu
from jax.sharding import PartitionSpec as P

LANES = 128
SUBS = 8
CHUNK = LANES * SUBS
AHEAD = 2
PAIR = 16
f32 = jnp.float32
bf16 = jnp.bfloat16


def stages(seq_n):
    radices, spans = [], []
    span = 1
    while span < seq_n:
        radices.append(min(4, seq_n // span))
        spans.append(span)
        span *= radices[-1]
    return radices, spans


def mixer_kernel(
    seq_n, chan_n, chunks, group_width,
    hid_h, qmr_h, kmr_h, vmr_h, qli_h, kli_h, filt_h, rate_h, resid_h, gain_h,
    out_h,
    hid, qmr, kmr, vmr, qli, kli, filt, rate_in, resid_in, ngain,
    spill, halo, outb, taps, upper, acc, src, rate, mgain,
    prefix, total, state_out, state_in, squares_out, squares_in,
    in_sem, par_sem, out_sem, halo_send, halo_recv,
    st_send, st_recv, sq_send, sq_recv,
):
    pos = lax.axis_index("seq")
    lane_pos = lax.axis_index("chan")
    tokens = hid.shape[1]
    modes = rate_in.shape[0]
    slab = modes * SUBS
    pitch = tokens + SUBS
    radices, spans = stages(seq_n)
    rounds = len(radices)
    per_block = LANES // group_width
    nxt = lax.rem(pos + 1, seq_n)
    prv = lax.rem(pos + seq_n - 1, seq_n)

    def cols(k):
        return pl.ds(k * CHUNK, CHUNK)

    pairs = ((kmr_h, kmr), (vmr_h, vmr), (qmr_h, qmr), (kli_h, kli), (hid_h, hid), (qli_h, qli))

    def in_copy(a, k):
        return pltpu.make_async_copy(pairs[a][0].at[:, cols(k)], pairs[a][1].at[k], in_sem.at[a, k])

    par_copies = [
        pltpu.make_async_copy(h, v, par_sem.at[i])
        for i, (h, v) in enumerate(
            ((filt_h, filt), (rate_h, rate_in), (resid_h, resid_in), (gain_h, ngain))
        )
    ]
    par_copies[0].start()
    for k in range(chunks):
        in_copy(0, k).start()
        in_copy(1, k).start()
    for c in par_copies[1:]:
        c.start()
    for a in range(2, 6):
        for k in range(chunks):
            in_copy(a, k).start()

    barrier = pltpu.get_barrier_semaphore()

    def greet(ids):
        pl.semaphore_signal(barrier, inc=1, device_id=ids, device_id_type=pl.DeviceIdType.MESH)

    greet({"seq": nxt})
    greet({"seq": prv})
    digits = [lax.rem(pos // m, q) for m, q in zip(spans, radices)]

    def member(r, e):
        return pos + spans[r] * (lax.rem(digits[r] + e, radices[r]) - digits[r])

    for r in range(rounds):
        for e in range(1, radices[r]):
            greet({"seq": member(r, e)})
    for d in range(1, chan_n):
        greet({"chan": lax.rem(lane_pos + d, chan_n)})

    def halo_copy(k):
        return pltpu.make_async_remote_copy(
            src_ref=spill.at[k], dst_ref=halo.at[k],
            send_sem=halo_send.at[k], recv_sem=halo_recv.at[k],
            device_id={"seq": nxt}, device_id_type=pl.DeviceIdType.MESH,
        )

    def state_copy(r, e, k):
        return pltpu.make_async_remote_copy(
            src_ref=state_out.at[r, k], dst_ref=state_in.at[r, e - 1, k],
            send_sem=st_send.at[r, e - 1, k], recv_sem=st_recv.at[r, e - 1, k],
            device_id={"seq": member(r, e)}, device_id_type=pl.DeviceIdType.MESH,
        )

    def squares_copy(d):
        return pltpu.make_async_remote_copy(
            src_ref=squares_out, dst_ref=squares_in.at[d - 1],
            send_sem=sq_send.at[d - 1], recv_sem=sq_recv.at[d - 1],
            device_id={"chan": lax.rem(lane_pos + d, chan_n)},
            device_id_type=pl.DeviceIdType.MESH,
        )

    def start_halo(k):
        pl.when(pos < seq_n - 1)(lambda: halo_copy(k).start())

    def halo_sent(k):
        pl.when(pos < seq_n - 1)(lambda: halo_copy(k).wait_send())

    @pl.when(pos == 0)
    def _():
        halo[...] = jnp.zeros_like(halo)

    in_copy(0, 0).wait()
    in_copy(1, 0).wait()
    spill[0] = (kmr[0].astype(f32) * vmr[0].astype(f32)).astype(bf16)
    pl.semaphore_wait(barrier, 2 + sum(radices) - rounds + chan_n - 1)
    start_halo(0)
    for c in par_copies:
        c.wait()

    tap_i = lax.broadcasted_iota(jnp.int32, (tokens, tokens), 0)
    pos_i = lax.broadcasted_iota(jnp.int32, (tokens, tokens), 1)
    wrap = jnp.where(lax.rem(tap_i + pos_i, tokens) == 0, 1.0, 0.0).astype(bf16)
    taps[...] = lax.dot_general(
        filt[...], wrap, (((0,), (0,)), ((), ())), preferred_element_type=f32
    )

    group_of_lane = lax.broadcasted_iota(jnp.int32, (tokens, LANES), 1) // group_width
    member_lanes = [jnp.where(group_of_lane == g, 1.0, 0.0).astype(bf16) for g in range(per_block)]

    def spread(x):
        return jnp.concatenate([x * m for m in member_lanes], 0)

    lags = lax.broadcasted_iota(jnp.int32, (tokens, LANES), 0) - lax.broadcasted_iota(
        jnp.int32, (tokens, LANES), 1
    )
    lower = jnp.where(lags >= 0, 1.0, 0.0).astype(bf16)
    higher = jnp.where(lags >= 0, 0.0, 1.0).astype(bf16)

    for k in range(chunks):
        if k > 0:
            in_copy(0, k).wait()
            in_copy(1, k).wait()

        def local_block(b, carry):
            j = k * SUBS + b
            lanes = pl.ds(pl.multiple_of(b * LANES, LANES), LANES)
            product = (kmr[k, :, lanes].astype(f32) * vmr[k, :, lanes].astype(f32)).astype(bf16)
            rows = taps[pl.ds(pl.multiple_of(j * per_block, per_block), per_block), :]
            own, over = [], []
            for g in range(per_block):
                first = pltpu.roll(
                    jnp.broadcast_to(rows[g : g + 1, :], (PAIR, LANES)),
                    0, 1, stride=1, stride_axis=0,
                ).astype(bf16)
                ring = jnp.concatenate(
                    [first] + [pltpu.roll(first, i, 1) for i in range(PAIR, tokens, PAIR)], 0
                )
                own.append(ring * lower)
                over.append(ring * higher)
            own, over = jnp.concatenate(own, 1), jnp.concatenate(over, 1)
            if k == 0:
                upper[b] = over
                acc[k, :, lanes] = jnp.dot(own, spread(product), preferred_element_type=f32)
            else:
                result = jnp.dot(
                    jnp.concatenate([own, over], 0), spread(product), preferred_element_type=f32
                )
                acc[k, :, lanes] = result[:tokens]
                spill[k, :, lanes] = result[tokens:].astype(bf16)
            return carry

        lax.fori_loop(0, SUBS, local_block, 0)
        if 0 < k < AHEAD:
            start_halo(k)

    for k in range(chunks):
        for b in range(SUBS):
            lanes = pl.ds(k * CHUNK + b * LANES, LANES)
            r = rate_in[:, lanes]
            x = 2.0 * r
            series = x * (
                1.0 - x * (1 / 2) * (1.0 - x * (1 / 3) * (1.0 - x * (1 / 4) * (
                    1.0 - x * (1 / 5) * (1.0 - x * (1 / 6) * (1.0 - x * (1 / 7))))))
            )
            grown = jnp.where(x < 0.1, series, 1.0 - jnp.exp(-x))
            rows = pl.ds(k * slab + b, modes, stride=SUBS)
            rate[rows, :] = r
            mgain[rows, :] = resid_in[:, lanes] * jnp.sqrt(grown)

    def chunk_rate(k):
        return rate[pl.ds(k * slab, slab), :]

    def chunk_mode(ref, k, n):
        return ref[pl.ds(k * slab + n * SUBS, SUBS), :]

    def medium_and_states(k):
        @pl.when(pos > 0)
        def _():
            halo_copy(k).wait_recv()

        for a in range(2, 5):
            in_copy(a, k).wait()

        def block(b, carry):
            j = k * SUBS + b
            lanes = pl.ds(pl.multiple_of(b * LANES, LANES), LANES)
            if k == 0:
                earlier = jnp.dot(
                    upper[b], spread(halo[k, :, lanes]), preferred_element_type=f32
                )
            else:
                earlier = halo[k, :, lanes].astype(f32)
            conv = acc[k, :, lanes] + earlier
            out_mr = (qmr[k, :, lanes].astype(f32) * conv).astype(bf16).astype(f32)
            src[pl.ds(pl.multiple_of(j * pitch, SUBS), tokens), :] = (
                kli[k, :, lanes].astype(f32) * out_mr
            )
            acc[k, :, lanes] = hid[k, :, lanes].astype(f32) + out_mr
            return carry

        lax.fori_loop(0, SUBS, block, 0)

        decay = [jnp.exp(-chunk_mode(rate, k, n)) for n in range(modes)]
        gain = [chunk_mode(mgain, k, n) for n in range(modes)]

        def end_step(t, states):
            x = src[pl.ds(k * SUBS * pitch + t, SUBS, stride=pitch), :]
            return tuple(decay[n] * states[n] + x for n in range(modes))

        def step(t, states):
            at = pl.ds(k * SUBS * pitch + t, SUBS, stride=pitch)
            x = src[at, :]
            states = tuple(decay[n] * states[n] + x for n in range(modes))
            parts = [gain[n] * states[n] for n in range(modes)]
            while len(parts) > 1:
                parts = [a + b for a, b in zip(parts[::2], parts[1::2])]
            src[at, :] = parts[0]
            return states

        zero = jnp.zeros((SUBS, LANES), f32)
        last = k == chunks - 1
        states = lax.fori_loop(
            0, tokens, end_step if last else step, (zero,) * modes, unroll=16
        )
        for n in range(modes):
            total[k, pl.ds(n * SUBS, SUBS), :] = states[n]
        prefix[k] = jnp.zeros((slab, LANES), f32)
        send_state(0, k)
        if last:
            lax.fori_loop(0, tokens, step, (zero,) * modes, unroll=16)

    def sends(r, e, act):
        if r < rounds - 1:
            act()
        else:
            pl.when(digits[r] + e < radices[r])(act)

    def takes(r, e, act):
        if r < rounds - 1:
            act()
        else:
            pl.when(digits[r] >= e)(act)

    def send_state(r, k):
        state_out[r, k] = total[k].astype(bf16)
        for e in range(1, radices[r]):
            sends(r, e, lambda: state_copy(r, e, k).start())

    def take_state(r, k):
        rates = chunk_rate(k)
        span, radix, digit = spans[r], radices[r], digits[r]
        inside = lax.rem(pos, span)

        def faded(steps, x):
            return jnp.exp(-rates * (tokens * steps).astype(f32)) * x

        if r < rounds - 1:
            total[k] = faded(span * (radix - 1 - digit), total[k])
        for e in range(1, radix):

            def take():
                state_copy(r, e, k).wait_recv()
                got = state_in[r, e - 1, k].astype(f32)
                sender = lax.rem(digit + radix - e, radix)
                earlier = sender < digit
                ahead = jnp.where(earlier, span * (digit - 1 - sender) + inside, 0)
                prefix[k] = prefix[k] + jnp.where(earlier, faded(ahead, got), 0.0)
                if r < rounds - 1:
                    total[k] = total[k] + faded(span * (radix - 1 - sender), got)

            takes(r, e, take)

    def finish_chunk(k):
        decay = [jnp.exp(-chunk_mode(rate, k, n)) for n in range(modes)]
        start = tuple(
            chunk_mode(mgain, k, n) * prefix[k, pl.ds(n * SUBS, SUBS), :] for n in range(modes)
        )

        def step(t, waves):
            at = pl.ds(k * SUBS * pitch + t, SUBS, stride=pitch)
            waves = tuple(decay[n] * waves[n] for n in range(modes))
            parts = list(waves)
            while len(parts) > 1:
                parts = [a + b for a, b in zip(parts[::2], parts[1::2])]
            src[at, :] = src[at, :] + parts[0]
            return waves

        lax.fori_loop(0, tokens, step, start, unroll=16)
        in_copy(5, k).wait()

        def block(b, carry):
            j = k * SUBS + b
            lanes = pl.ds(pl.multiple_of(b * LANES, LANES), LANES)
            conv = src[pl.ds(pl.multiple_of(j * pitch, SUBS), tokens), :]
            combined = acc[k, :, lanes] + qli[k, :, lanes].astype(f32) * conv
            acc[k, :, lanes] = combined
            squares_out[...] += combined * combined
            return carry

        lax.fori_loop(0, SUBS, block, 0)

    squares_out[...] = jnp.zeros_like(squares_out)
    for turn in range(chunks + rounds):
        if turn < chunks:
            halo_sent(turn)
            if turn + AHEAD < chunks:
                start_halo(turn + AHEAD)
            medium_and_states(turn)
        for k in range(chunks):
            r = turn - k - 1
            if 0 <= r < rounds:
                take_state(r, k)
                if r + 1 < rounds:
                    send_state(r + 1, k)
        done = turn - rounds
        if 0 <= done < chunks:
            finish_chunk(done)

    sums = squares_out[...]
    for d in range(1, chan_n):
        squares_copy(d).start()
    for d in range(1, chan_n):
        squares_copy(d).wait_recv()
        sums = sums + squares_in[d - 1]
    width = chunks * CHUNK * chan_n
    inverse = lax.rsqrt(jnp.sum(sums, 1, keepdims=True) / width + 1e-06)

    for k in range(chunks):
        outb[k] = (acc[k] * inverse * ngain[:, cols(k)]).astype(bf16)
        pltpu.make_async_copy(outb.at[k], out_h.at[:, cols(k)], out_sem.at[k]).start()

    for k in range(chunks):
        pltpu.make_async_copy(outb.at[k], out_h.at[:, cols(k)], out_sem.at[k]).wait()

        for r in range(rounds):
            for e in range(1, radices[r]):
                sends(r, e, lambda: state_copy(r, e, k).wait_send())

    for d in range(1, chan_n):
        squares_copy(d).wait_send()


def per_device(
    seq_n, chan_n,
    hidden_in, query_mr, key_mr, value_mr, query_li, key_li,
    mr_filter, li_rate, li_residue, norm_gain,
):
    tokens, channels = hidden_in.shape
    groups = mr_filter.shape[1]
    modes = li_rate.shape[0]
    chunks = channels // CHUNK
    radices, _ = stages(seq_n)
    rounds, most = len(radices), max(radices) - 1
    slab = modes * SUBS
    assert seq_n & (seq_n - 1) == 0 and tokens == mr_filter.shape[0] == LANES
    big = pltpu.VMEM((chunks, tokens, CHUNK), bf16)
    dma = pltpu.SemaphoreType.DMA
    return pl.pallas_call(
        functools.partial(mixer_kernel, seq_n, chan_n, chunks, channels // groups),
        out_shape=jax.ShapeDtypeStruct((tokens, channels), bf16),
        in_specs=[pl.BlockSpec(memory_space=pl.ANY)] * 10,
        out_specs=pl.BlockSpec(memory_space=pl.ANY),
        scratch_shapes=[
            big, big, big, big, big, big,
            pltpu.VMEM(mr_filter.shape, bf16),
            pltpu.VMEM(li_rate.shape, f32),
            pltpu.VMEM(li_residue.shape, f32),
            pltpu.VMEM((1, channels), f32),
            big, big, big,
            pltpu.VMEM((groups, tokens), f32),
            pltpu.VMEM((SUBS, tokens, tokens * LANES * groups // channels), bf16),
            pltpu.VMEM((chunks, tokens, CHUNK), f32),
            pltpu.VMEM((channels // LANES * (tokens + SUBS), LANES), f32),
            pltpu.VMEM((chunks * slab, LANES), f32),
            pltpu.VMEM((chunks * slab, LANES), f32),
            pltpu.VMEM((chunks, slab, LANES), f32),
            pltpu.VMEM((chunks, slab, LANES), f32),
            pltpu.VMEM((rounds, chunks, slab, LANES), bf16),
            pltpu.VMEM((rounds, most, chunks, slab, LANES), bf16),
            pltpu.VMEM((tokens, LANES), f32),
            pltpu.VMEM((max(chan_n - 1, 1), tokens, LANES), f32),
            dma((6, chunks)),
            dma((4,)),
            dma((chunks,)),
            dma((chunks,)),
            dma((chunks,)),
            dma((rounds, most, chunks)),
            dma((rounds, most, chunks)),
            dma((max(chan_n - 1, 1),)),
            dma((max(chan_n - 1, 1),)),
        ],
        compiler_params=pltpu.CompilerParams(
            collective_id=0, has_side_effects=True, vmem_limit_bytes=63 * 1024 * 1024
        ),
        cost_estimate=pl.CostEstimate(
            flops=4 * tokens * tokens * channels * LANES * groups // channels,
            bytes_accessed=14 * tokens * channels,
            transcendentals=4 * modes * channels,
        ),
        name="hyena_mixers",
    )(
        hidden_in, query_mr, key_mr, value_mr, query_li, key_li,
        mr_filter, li_rate, li_residue, norm_gain.reshape(1, channels),
    )


def solution(mesh):
    seq_n, chan_n = mesh.shape["seq"], mesh.shape["chan"]
    rows = P("seq", "chan")
    by_channel = P(None, "chan")
    in_specs = (rows,) * 6 + (by_channel,) * 3 + (P("chan"),)
    return jax.shard_map(
        functools.partial(per_device, seq_n, chan_n),
        mesh=mesh, in_specs=in_specs, out_specs=rows, check_vma=False,
    )
```

```python
import functools

import jax
import jax.numpy as jnp
from jax import lax
from jax.experimental import pallas as pl
from jax.experimental.pallas import tpu as pltpu
from jax.sharding import PartitionSpec as P

LANES = 128
SUBS = 8
CHUNK = LANES * SUBS
AHEAD = 2
PAIR = 16
GROUP = 8
f32 = jnp.float32
bf16 = jnp.bfloat16


def stages(seq_n):
    radices, spans = [], []
    span = 1
    while span < seq_n:
        radices.append(min(4, seq_n // span))
        spans.append(span)
        span *= radices[-1]
    return radices, spans


def mixer_kernel(
    seq_n, chan_n, chunks, group_width,
    hid_h, qmr_h, kmr_h, vmr_h, qli_h, kli_h, filt_h, rate_h, resid_h, gain_h,
    out_h,
    hid, qmr, kmr, vmr, qli, kli, filt, rate_in, resid_in, ngain,
    spill, halo, outb, taps, upper, acc, src, own_li, rate, fade, mgain,
    prefix, total, state_out, state_in, squares_out, squares_in,
    in_sem, par_sem, out_sem, halo_send, halo_recv,
    st_send, st_recv, sq_send, sq_recv,
):
    pos = lax.axis_index("seq")
    lane_pos = lax.axis_index("chan")
    tokens = hid.shape[1]
    modes = rate_in.shape[0]
    slab = modes * SUBS
    pitch = tokens + SUBS
    radices, spans = stages(seq_n)
    rounds = len(radices)
    per_block = LANES // group_width
    nxt = lax.rem(pos + 1, seq_n)
    prv = lax.rem(pos + seq_n - 1, seq_n)

    def cols(k):
        return pl.ds(k * CHUNK, CHUNK)

    pairs = ((kmr_h, kmr), (vmr_h, vmr), (qmr_h, qmr), (kli_h, kli), (hid_h, hid), (qli_h, qli))

    def in_copy(a, k):
        return pltpu.make_async_copy(pairs[a][0].at[:, cols(k)], pairs[a][1].at[k], in_sem.at[a, k])

    par_copies = [
        pltpu.make_async_copy(h, v, par_sem.at[i])
        for i, (h, v) in enumerate(
            ((filt_h, filt), (rate_h, rate_in), (resid_h, resid_in), (gain_h, ngain))
        )
    ]
    par_copies[0].start()
    for k in range(chunks):
        in_copy(0, k).start()
        in_copy(1, k).start()
    for c in par_copies[1:]:
        c.start()
    for a in range(2, 6):
        for k in range(chunks):
            in_copy(a, k).start()

    barrier = pltpu.get_barrier_semaphore()

    def greet(ids):
        pl.semaphore_signal(barrier, inc=1, device_id=ids, device_id_type=pl.DeviceIdType.MESH)

    greet({"seq": nxt})
    greet({"seq": prv})
    digits = [lax.rem(pos // m, q) for m, q in zip(spans, radices)]

    def member(r, e):
        return pos + spans[r] * (lax.rem(digits[r] + e, radices[r]) - digits[r])

    for r in range(rounds):
        for e in range(1, radices[r]):
            greet({"seq": member(r, e)})
    for d in range(1, chan_n):
        greet({"chan": lax.rem(lane_pos + d, chan_n)})

    def halo_copy(k):
        return pltpu.make_async_remote_copy(
            src_ref=spill.at[k], dst_ref=halo.at[k],
            send_sem=halo_send.at[k], recv_sem=halo_recv.at[k],
            device_id={"seq": nxt}, device_id_type=pl.DeviceIdType.MESH,
        )

    def state_copy(r, e, k):
        return pltpu.make_async_remote_copy(
            src_ref=state_out.at[r, k], dst_ref=state_in.at[r, e - 1, k],
            send_sem=st_send.at[r, e - 1, k], recv_sem=st_recv.at[r, e - 1, k],
            device_id={"seq": member(r, e)}, device_id_type=pl.DeviceIdType.MESH,
        )

    def squares_copy(d):
        return pltpu.make_async_remote_copy(
            src_ref=squares_out, dst_ref=squares_in.at[d - 1],
            send_sem=sq_send.at[d - 1], recv_sem=sq_recv.at[d - 1],
            device_id={"chan": lax.rem(lane_pos + d, chan_n)},
            device_id_type=pl.DeviceIdType.MESH,
        )

    def start_halo(k):
        pl.when(pos < seq_n - 1)(lambda: halo_copy(k).start())

    def halo_sent(k):
        pl.when(pos < seq_n - 1)(lambda: halo_copy(k).wait_send())

    @pl.when(pos == 0)
    def _():
        halo[...] = jnp.zeros_like(halo)

    in_copy(0, 0).wait()
    in_copy(1, 0).wait()
    spill[0] = (kmr[0].astype(f32) * vmr[0].astype(f32)).astype(bf16)
    pl.semaphore_wait(barrier, 2 + sum(radices) - rounds + chan_n - 1)
    start_halo(0)
    for c in par_copies:
        c.wait()

    tap_i = lax.broadcasted_iota(jnp.int32, (tokens, tokens), 0)
    pos_i = lax.broadcasted_iota(jnp.int32, (tokens, tokens), 1)
    wrap = jnp.where(lax.rem(tap_i + pos_i, tokens) == 0, 1.0, 0.0).astype(bf16)
    taps[...] = lax.dot_general(
        filt[...], wrap, (((0,), (0,)), ((), ())), preferred_element_type=f32
    )

    group_of_lane = lax.broadcasted_iota(jnp.int32, (tokens, LANES), 1) // group_width
    member_lanes = [jnp.where(group_of_lane == g, 1.0, 0.0).astype(bf16) for g in range(per_block)]

    def spread(x):
        return jnp.concatenate([x * m for m in member_lanes], 0)

    lags = lax.broadcasted_iota(jnp.int32, (tokens, LANES), 0) - lax.broadcasted_iota(
        jnp.int32, (tokens, LANES), 1
    )
    lower = jnp.where(lags >= 0, 1.0, 0.0).astype(bf16)
    higher = jnp.where(lags >= 0, 0.0, 1.0).astype(bf16)

    for k in range(chunks):
        if k > 0:
            in_copy(0, k).wait()
            in_copy(1, k).wait()

        def local_block(b, carry):
            j = k * SUBS + b
            lanes = pl.ds(pl.multiple_of(b * LANES, LANES), LANES)
            product = (kmr[k, :, lanes].astype(f32) * vmr[k, :, lanes].astype(f32)).astype(bf16)
            rows = taps[pl.ds(pl.multiple_of(j * per_block, per_block), per_block), :]
            own, over = [], []
            for g in range(per_block):
                first = pltpu.roll(
                    jnp.broadcast_to(rows[g : g + 1, :], (PAIR, LANES)),
                    0, 1, stride=1, stride_axis=0,
                ).astype(bf16)
                ring = jnp.concatenate(
                    [first] + [pltpu.roll(first, i, 1) for i in range(PAIR, tokens, PAIR)], 0
                )
                own.append(ring * lower)
                over.append(ring * higher)
            own, over = jnp.concatenate(own, 1), jnp.concatenate(over, 1)
            if k == 0:
                upper[b] = over
                acc[k, :, lanes] = jnp.dot(own, spread(product), preferred_element_type=f32)
            else:
                result = jnp.dot(
                    jnp.concatenate([own, over], 0), spread(product), preferred_element_type=f32
                )
                acc[k, :, lanes] = result[:tokens]
                spill[k, :, lanes] = result[tokens:].astype(bf16)
            return carry

        lax.fori_loop(0, SUBS, local_block, 0)
        if 0 < k < AHEAD:
            start_halo(k)

    for k in range(chunks):
        for b in range(SUBS):
            lanes = pl.ds(k * CHUNK + b * LANES, LANES)
            r = rate_in[:, lanes]
            x = 2.0 * r
            series = x * (
                1.0 - x * (1 / 2) * (1.0 - x * (1 / 3) * (1.0 - x * (1 / 4) * (
                    1.0 - x * (1 / 5) * (1.0 - x * (1 / 6) * (1.0 - x * (1 / 7))))))
            )
            grown = jnp.where(x < 0.1, series, 1.0 - jnp.exp(-x))
            rows = pl.ds(k * slab + b, modes, stride=SUBS)
            rate[rows, :] = r
            fade[rows, :] = jnp.exp(-r)
            mgain[rows, :] = resid_in[:, lanes] * jnp.sqrt(grown)

    def chunk_rate(k):
        return rate[pl.ds(k * slab, slab), :]

    def chunk_mode(ref, k, n):
        return ref[pl.ds(k * slab + n * SUBS, SUBS), :]

    def at_token(k, i, u):
        return pl.ds(k * SUBS * pitch + i * GROUP + u, SUBS, stride=pitch)

    def medium_and_states(k):
        @pl.when(pos > 0)
        def _():
            halo_copy(k).wait_recv()

        for a in range(2, 5):
            in_copy(a, k).wait()

        def block(b, carry):
            j = k * SUBS + b
            lanes = pl.ds(pl.multiple_of(b * LANES, LANES), LANES)
            if k == 0:
                earlier = jnp.dot(
                    upper[b], spread(halo[k, :, lanes]), preferred_element_type=f32
                )
            else:
                earlier = halo[k, :, lanes].astype(f32)
            conv = acc[k, :, lanes] + earlier
            out_mr = (qmr[k, :, lanes].astype(f32) * conv).astype(bf16).astype(f32)
            src[pl.ds(pl.multiple_of(j * pitch, SUBS), tokens), :] = (
                kli[k, :, lanes].astype(f32) * out_mr
            )
            acc[k, :, lanes] = hid[k, :, lanes].astype(f32) + out_mr
            return carry

        lax.fori_loop(0, SUBS, block, 0)

        def end_step(i, states):
            xs = [src[at_token(k, i, u), :] for u in range(GROUP)]
            ends = []
            for n in range(modes):
                decay, state = chunk_mode(fade, k, n), states[n]
                for x in xs:
                    state = decay * state + x
                ends.append(state)
            return tuple(ends)

        def step(i, states):
            xs = [src[at_token(k, i, u), :] for u in range(GROUP)]
            sums, ends = [None] * GROUP, []
            for n in range(modes):
                decay, gain, state = chunk_mode(fade, k, n), chunk_mode(mgain, k, n), states[n]
                for u, x in enumerate(xs):
                    state = decay * state + x
                    part = gain * state
                    sums[u] = part if n == 0 else sums[u] + part
                ends.append(state)
            for u in range(GROUP):
                own_li[at_token(k, i, u), :] = sums[u]
            return tuple(ends)

        zero = jnp.zeros((SUBS, LANES), f32)
        last = k == chunks - 1
        states = lax.fori_loop(
            0, tokens // GROUP, end_step if last else step, (zero,) * modes, unroll=2
        )
        for n in range(modes):
            total[k, pl.ds(n * SUBS, SUBS), :] = states[n]
        prefix[k] = jnp.zeros((slab, LANES), f32)
        send_state(0, k)
        if last:
            lax.fori_loop(0, tokens // GROUP, step, (zero,) * modes, unroll=2)

    def sends(r, e, act):
        if r < rounds - 1:
            act()
        else:
            pl.when(digits[r] + e < radices[r])(act)

    def takes(r, e, act):
        if r < rounds - 1:
            act()
        else:
            pl.when(digits[r] >= e)(act)

    def send_state(r, k):
        state_out[r, k] = total[k].astype(bf16)
        for e in range(1, radices[r]):
            sends(r, e, lambda: state_copy(r, e, k).start())

    def take_state(r, k):
        rates = chunk_rate(k)
        span, radix, digit = spans[r], radices[r], digits[r]
        inside = lax.rem(pos, span)

        def faded(steps, x):
            return jnp.exp(-rates * (tokens * steps).astype(f32)) * x

        if r < rounds - 1:
            total[k] = faded(span * (radix - 1 - digit), total[k])
        for e in range(1, radix):

            def take():
                state_copy(r, e, k).wait_recv()
                got = state_in[r, e - 1, k].astype(f32)
                sender = lax.rem(digit + radix - e, radix)
                earlier = sender < digit
                ahead = jnp.where(earlier, span * (digit - 1 - sender) + inside, 0)
                prefix[k] = prefix[k] + jnp.where(earlier, faded(ahead, got), 0.0)
                if r < rounds - 1:
                    total[k] = total[k] + faded(span * (radix - 1 - sender), got)

            takes(r, e, take)

    def finish_chunk(k):
        start = tuple(
            chunk_mode(mgain, k, n) * prefix[k, pl.ds(n * SUBS, SUBS), :] for n in range(modes)
        )

        def step(i, waves):
            sums, ends = [own_li[at_token(k, i, u), :] for u in range(GROUP)], []
            for n in range(modes):
                decay, wave = chunk_mode(fade, k, n), waves[n]
                for u in range(GROUP):
                    wave = decay * wave
                    sums[u] = sums[u] + wave
                ends.append(wave)
            for u in range(GROUP):
                own_li[at_token(k, i, u), :] = sums[u]
            return tuple(ends)

        lax.fori_loop(0, tokens // GROUP, step, start, unroll=2)
        in_copy(5, k).wait()

        def block(b, carry):
            j = k * SUBS + b
            lanes = pl.ds(pl.multiple_of(b * LANES, LANES), LANES)
            conv = own_li[pl.ds(pl.multiple_of(j * pitch, SUBS), tokens), :]
            combined = acc[k, :, lanes] + qli[k, :, lanes].astype(f32) * conv
            acc[k, :, lanes] = combined
            squares_out[...] += combined * combined
            return carry

        lax.fori_loop(0, SUBS, block, 0)

    squares_out[...] = jnp.zeros_like(squares_out)
    for turn in range(chunks + rounds):
        if turn < chunks:
            halo_sent(turn)
            if turn + AHEAD < chunks:
                start_halo(turn + AHEAD)
            medium_and_states(turn)
        for k in range(chunks):
            r = turn - k - 1
            if 0 <= r < rounds:
                take_state(r, k)
                if r + 1 < rounds:
                    send_state(r + 1, k)
        done = turn - rounds
        if 0 <= done < chunks:
            finish_chunk(done)

    sums = squares_out[...]
    for d in range(1, chan_n):
        squares_copy(d).start()
    for d in range(1, chan_n):
        squares_copy(d).wait_recv()
        sums = sums + squares_in[d - 1]
    width = chunks * CHUNK * chan_n
    inverse = lax.rsqrt(jnp.sum(sums, 1, keepdims=True) / width + 1e-06)

    for k in range(chunks):
        outb[k] = (acc[k] * inverse * ngain[:, cols(k)]).astype(bf16)
        pltpu.make_async_copy(outb.at[k], out_h.at[:, cols(k)], out_sem.at[k]).start()

    for k in range(chunks):
        pltpu.make_async_copy(outb.at[k], out_h.at[:, cols(k)], out_sem.at[k]).wait()

        for r in range(rounds):
            for e in range(1, radices[r]):
                sends(r, e, lambda: state_copy(r, e, k).wait_send())

    for d in range(1, chan_n):
        squares_copy(d).wait_send()


def per_device(
    seq_n, chan_n,
    hidden_in, query_mr, key_mr, value_mr, query_li, key_li,
    mr_filter, li_rate, li_residue, norm_gain,
):
    tokens, channels = hidden_in.shape
    groups = mr_filter.shape[1]
    modes = li_rate.shape[0]
    chunks = channels // CHUNK
    radices, _ = stages(seq_n)
    rounds, most = len(radices), max(radices) - 1
    slab = modes * SUBS
    assert seq_n & (seq_n - 1) == 0 and tokens == mr_filter.shape[0] == LANES
    big = pltpu.VMEM((chunks, tokens, CHUNK), bf16)
    dma = pltpu.SemaphoreType.DMA
    return pl.pallas_call(
        functools.partial(mixer_kernel, seq_n, chan_n, chunks, channels // groups),
        out_shape=jax.ShapeDtypeStruct((tokens, channels), bf16),
        in_specs=[pl.BlockSpec(memory_space=pl.ANY)] * 10,
        out_specs=pl.BlockSpec(memory_space=pl.ANY),
        scratch_shapes=[
            big, big, big, big, big, big,
            pltpu.VMEM(mr_filter.shape, bf16),
            pltpu.VMEM(li_rate.shape, f32),
            pltpu.VMEM(li_residue.shape, f32),
            pltpu.VMEM((1, channels), f32),
            big, big, big,
            pltpu.VMEM((groups, tokens), f32),
            pltpu.VMEM((SUBS, tokens, tokens * LANES * groups // channels), bf16),
            pltpu.VMEM((chunks, tokens, CHUNK), f32),
            pltpu.VMEM((channels // LANES * (tokens + SUBS), LANES), f32),
            pltpu.VMEM((channels // LANES * (tokens + SUBS), LANES), f32),
            pltpu.VMEM((chunks * slab, LANES), f32),
            pltpu.VMEM((chunks * slab, LANES), f32),
            pltpu.VMEM((chunks * slab, LANES), f32),
            pltpu.VMEM((chunks, slab, LANES), f32),
            pltpu.VMEM((chunks, slab, LANES), f32),
            pltpu.VMEM((rounds, chunks, slab, LANES), bf16),
            pltpu.VMEM((rounds, most, chunks, slab, LANES), bf16),
            pltpu.VMEM((tokens, LANES), f32),
            pltpu.VMEM((max(chan_n - 1, 1), tokens, LANES), f32),
            dma((6, chunks)),
            dma((4,)),
            dma((chunks,)),
            dma((chunks,)),
            dma((chunks,)),
            dma((rounds, most, chunks)),
            dma((rounds, most, chunks)),
            dma((max(chan_n - 1, 1),)),
            dma((max(chan_n - 1, 1),)),
        ],
        compiler_params=pltpu.CompilerParams(
            collective_id=0, has_side_effects=True, vmem_limit_bytes=63 * 1024 * 1024
        ),
        cost_estimate=pl.CostEstimate(
            flops=4 * tokens * tokens * channels * LANES * groups // channels,
            bytes_accessed=14 * tokens * channels,
            transcendentals=4 * modes * channels,
        ),
        name="hyena_mixers",
    )(
        hidden_in, query_mr, key_mr, value_mr, query_li, key_li,
        mr_filter, li_rate, li_residue, norm_gain.reshape(1, channels),
    )


def solution(mesh):
    seq_n, chan_n = mesh.shape["seq"], mesh.shape["chan"]
    rows = P("seq", "chan")
    by_channel = P(None, "chan")
    in_specs = (rows,) * 6 + (by_channel,) * 3 + (P("chan"),)
    return jax.shard_map(
        functools.partial(per_device, seq_n, chan_n),
        mesh=mesh, in_specs=in_specs, out_specs=rows, check_vma=False,
    )
```

```python
import functools

import jax
import jax.numpy as jnp
from jax import lax
from jax.experimental import pallas as pl
from jax.experimental.pallas import tpu as pltpu
from jax.sharding import PartitionSpec as P

LANES = 128
SUBS = 8
CHUNK = LANES * SUBS
AHEAD = 4
PAIR = 16
GROUP = 8
f32 = jnp.float32
bf16 = jnp.bfloat16


def stages(seq_n):
    radices, spans = [], []
    span = 1
    while span < seq_n:
        radices.append(min(4, seq_n // span))
        spans.append(span)
        span *= radices[-1]
    return radices, spans


def mixer_kernel(
    seq_n, chan_n, chunks, group_width,
    hid_h, qmr_h, kmr_h, vmr_h, qli_h, kli_h, filt_h, rate_h, resid_h, gain_h,
    out_h,
    hid, qmr, kmr, vmr, qli, kli, filt, rate_in, resid_in, ngain,
    spill, halo, outb, taps, upper, acc, src, own_li, rate, fade, mgain,
    prefix, total, state_out, state_in, squares_out, squares_in,
    in_sem, par_sem, out_sem, halo_send, halo_recv,
    st_send, st_recv, sq_send, sq_recv,
):
    pos = lax.axis_index("seq")
    lane_pos = lax.axis_index("chan")
    tokens = hid.shape[1]
    modes = rate_in.shape[0]
    slab = modes * SUBS
    pitch = tokens + SUBS
    radices, spans = stages(seq_n)
    rounds = len(radices)
    per_block = LANES // group_width
    nxt = lax.rem(pos + 1, seq_n)
    prv = lax.rem(pos + seq_n - 1, seq_n)

    def cols(k):
        return pl.ds(k * CHUNK, CHUNK)

    pairs = ((kmr_h, kmr), (vmr_h, vmr), (qmr_h, qmr), (kli_h, kli), (hid_h, hid), (qli_h, qli))

    def in_copy(a, k):
        return pltpu.make_async_copy(pairs[a][0].at[:, cols(k)], pairs[a][1].at[k], in_sem.at[a, k])

    par_copies = [
        pltpu.make_async_copy(h, v, par_sem.at[i])
        for i, (h, v) in enumerate(
            ((filt_h, filt), (rate_h, rate_in), (resid_h, resid_in), (gain_h, ngain))
        )
    ]
    par_copies[0].start()
    for k in range(chunks):
        in_copy(0, k).start()
        in_copy(1, k).start()
    for c in par_copies[1:]:
        c.start()
    for a in range(2, 6):
        for k in range(chunks):
            in_copy(a, k).start()

    barrier = pltpu.get_barrier_semaphore()

    def greet(ids):
        pl.semaphore_signal(barrier, inc=1, device_id=ids, device_id_type=pl.DeviceIdType.MESH)

    greet({"seq": nxt})
    greet({"seq": prv})
    digits = [lax.rem(pos // m, q) for m, q in zip(spans, radices)]

    def member(r, e):
        return pos + spans[r] * (lax.rem(digits[r] + e, radices[r]) - digits[r])

    for r in range(rounds):
        for e in range(1, radices[r]):
            greet({"seq": member(r, e)})
    for d in range(1, chan_n):
        greet({"chan": lax.rem(lane_pos + d, chan_n)})

    def halo_copy(k):
        return pltpu.make_async_remote_copy(
            src_ref=spill.at[k], dst_ref=halo.at[k],
            send_sem=halo_send.at[k], recv_sem=halo_recv.at[k],
            device_id={"seq": nxt}, device_id_type=pl.DeviceIdType.MESH,
        )

    def state_copy(r, e, k):
        return pltpu.make_async_remote_copy(
            src_ref=state_out.at[r, k], dst_ref=state_in.at[r, e - 1, k],
            send_sem=st_send.at[r, e - 1, k], recv_sem=st_recv.at[r, e - 1, k],
            device_id={"seq": member(r, e)}, device_id_type=pl.DeviceIdType.MESH,
        )

    def squares_copy(d):
        return pltpu.make_async_remote_copy(
            src_ref=squares_out, dst_ref=squares_in.at[d - 1],
            send_sem=sq_send.at[d - 1], recv_sem=sq_recv.at[d - 1],
            device_id={"chan": lax.rem(lane_pos + d, chan_n)},
            device_id_type=pl.DeviceIdType.MESH,
        )

    def start_halo(k):
        pl.when(pos < seq_n - 1)(lambda: halo_copy(k).start())

    def halo_sent(k):
        pl.when(pos < seq_n - 1)(lambda: halo_copy(k).wait_send())

    @pl.when(pos == 0)
    def _():
        halo[...] = jnp.zeros_like(halo)

    in_copy(0, 0).wait()
    in_copy(1, 0).wait()
    spill[0] = (kmr[0].astype(f32) * vmr[0].astype(f32)).astype(bf16)
    pl.semaphore_wait(barrier, 2 + sum(radices) - rounds + chan_n - 1)
    start_halo(0)
    for c in par_copies:
        c.wait()

    tap_i = lax.broadcasted_iota(jnp.int32, (tokens, tokens), 0)
    pos_i = lax.broadcasted_iota(jnp.int32, (tokens, tokens), 1)
    wrap = jnp.where(lax.rem(tap_i + pos_i, tokens) == 0, 1.0, 0.0).astype(bf16)
    taps[...] = lax.dot_general(
        filt[...], wrap, (((0,), (0,)), ((), ())), preferred_element_type=f32
    )

    group_of_lane = lax.broadcasted_iota(jnp.int32, (tokens, LANES), 1) // group_width
    member_lanes = [jnp.where(group_of_lane == g, 1.0, 0.0).astype(bf16) for g in range(per_block)]

    def spread(x):
        return jnp.concatenate([x * m for m in member_lanes], 0)

    lags = lax.broadcasted_iota(jnp.int32, (tokens, LANES), 0) - lax.broadcasted_iota(
        jnp.int32, (tokens, LANES), 1
    )
    lower = jnp.where(lags >= 0, 1.0, 0.0).astype(bf16)
    higher = jnp.where(lags >= 0, 0.0, 1.0).astype(bf16)

    for k in range(chunks):
        if k > 0:
            in_copy(0, k).wait()
            in_copy(1, k).wait()

        def local_block(b, carry):
            j = k * SUBS + b
            lanes = pl.ds(pl.multiple_of(b * LANES, LANES), LANES)
            product = (kmr[k, :, lanes].astype(f32) * vmr[k, :, lanes].astype(f32)).astype(bf16)
            rows = taps[pl.ds(pl.multiple_of(j * per_block, per_block), per_block), :]
            own, over = [], []
            for g in range(per_block):
                first = pltpu.roll(
                    jnp.broadcast_to(rows[g : g + 1, :], (PAIR, LANES)),
                    0, 1, stride=1, stride_axis=0,
                ).astype(bf16)
                ring = jnp.concatenate(
                    [first] + [pltpu.roll(first, i, 1) for i in range(PAIR, tokens, PAIR)], 0
                )
                own.append(ring * lower)
                over.append(ring * higher)
            own, over = jnp.concatenate(own, 1), jnp.concatenate(over, 1)
            if k == 0:
                upper[b] = over
                acc[k, :, lanes] = jnp.dot(own, spread(product), preferred_element_type=f32)
            else:
                result = jnp.dot(
                    jnp.concatenate([own, over], 0), spread(product), preferred_element_type=f32
                )
                acc[k, :, lanes] = result[:tokens]
                spill[k, :, lanes] = result[tokens:].astype(bf16)
            return carry

        lax.fori_loop(0, SUBS, local_block, 0)
        if 0 < k < AHEAD:
            start_halo(k)

    for k in range(chunks):
        for b in range(SUBS):
            lanes = pl.ds(k * CHUNK + b * LANES, LANES)
            r = rate_in[:, lanes]
            x = 2.0 * r
            series = x * (
                1.0 - x * (1 / 2) * (1.0 - x * (1 / 3) * (1.0 - x * (1 / 4) * (
                    1.0 - x * (1 / 5) * (1.0 - x * (1 / 6) * (1.0 - x * (1 / 7))))))
            )
            grown = jnp.where(x < 0.1, series, 1.0 - jnp.exp(-x))
            rows = pl.ds(k * slab + b, modes, stride=SUBS)
            rate[rows, :] = r
            fade[rows, :] = jnp.exp(-r)
            mgain[rows, :] = resid_in[:, lanes] * jnp.sqrt(grown)

    def chunk_rate(k):
        return rate[pl.ds(k * slab, slab), :]

    def chunk_mode(ref, k, n):
        return ref[pl.ds(k * slab + n * SUBS, SUBS), :]

    def at_token(k, i, u):
        return pl.ds(k * SUBS * pitch + i * GROUP + u, SUBS, stride=pitch)

    def medium_and_states(k):
        @pl.when(pos > 0)
        def _():
            halo_copy(k).wait_recv()

        for a in range(2, 5):
            in_copy(a, k).wait()

        def block(b, carry):
            j = k * SUBS + b
            lanes = pl.ds(pl.multiple_of(b * LANES, LANES), LANES)
            if k == 0:
                earlier = jnp.dot(
                    upper[b], spread(halo[k, :, lanes]), preferred_element_type=f32
                )
            else:
                earlier = halo[k, :, lanes].astype(f32)
            conv = acc[k, :, lanes] + earlier
            out_mr = (qmr[k, :, lanes].astype(f32) * conv).astype(bf16).astype(f32)
            src[pl.ds(pl.multiple_of(j * pitch, SUBS), tokens), :] = (
                kli[k, :, lanes].astype(f32) * out_mr
            )
            acc[k, :, lanes] = hid[k, :, lanes].astype(f32) + out_mr
            return carry

        lax.fori_loop(0, SUBS, block, 0)

        def end_step(i, states):
            xs = [src[at_token(k, i, u), :] for u in range(GROUP)]
            ends = []
            for n in range(modes):
                decay, state = chunk_mode(fade, k, n), states[n]
                for x in xs:
                    state = decay * state + x
                ends.append(state)
            return tuple(ends)

        def step(i, states):
            xs = [src[at_token(k, i, u), :] for u in range(GROUP)]
            sums, ends = [None] * GROUP, []
            for n in range(modes):
                decay, gain, state = chunk_mode(fade, k, n), chunk_mode(mgain, k, n), states[n]
                for u, x in enumerate(xs):
                    state = decay * state + x
                    part = gain * state
                    sums[u] = part if n == 0 else sums[u] + part
                ends.append(state)
            for u in range(GROUP):
                own_li[at_token(k, i, u), :] = sums[u]
            return tuple(ends)

        zero = jnp.zeros((SUBS, LANES), f32)
        last = k == chunks - 1
        states = lax.fori_loop(
            0, tokens // GROUP, end_step if last else step, (zero,) * modes, unroll=2
        )
        for n in range(modes):
            total[k, pl.ds(n * SUBS, SUBS), :] = states[n]
        prefix[k] = jnp.zeros((slab, LANES), f32)
        send_state(0, k)
        if last:
            lax.fori_loop(0, tokens // GROUP, step, (zero,) * modes, unroll=2)

    def sends(r, e, act):
        if r < rounds - 1:
            act()
        else:
            pl.when(digits[r] + e < radices[r])(act)

    def takes(r, e, act):
        if r < rounds - 1:
            act()
        else:
            pl.when(digits[r] >= e)(act)

    def send_state(r, k):
        state_out[r, k] = total[k].astype(bf16)
        for e in range(1, radices[r]):
            sends(r, e, lambda: state_copy(r, e, k).start())

    def take_state(r, k):
        rates = chunk_rate(k)
        span, radix, digit = spans[r], radices[r], digits[r]
        inside = lax.rem(pos, span)

        def faded(steps, x):
            return jnp.exp(-rates * (tokens * steps).astype(f32)) * x

        if r < rounds - 1:
            total[k] = faded(span * (radix - 1 - digit), total[k])
        for e in range(1, radix):

            def take():
                state_copy(r, e, k).wait_recv()
                got = state_in[r, e - 1, k].astype(f32)
                sender = lax.rem(digit + radix - e, radix)
                earlier = sender < digit
                ahead = jnp.where(earlier, span * (digit - 1 - sender) + inside, 0)
                prefix[k] = prefix[k] + jnp.where(earlier, faded(ahead, got), 0.0)
                if r < rounds - 1:
                    total[k] = total[k] + faded(span * (radix - 1 - sender), got)

            takes(r, e, take)

    def finish_chunk(k):
        start = tuple(
            chunk_mode(mgain, k, n) * prefix[k, pl.ds(n * SUBS, SUBS), :] for n in range(modes)
        )

        def step(i, waves):
            sums, ends = [own_li[at_token(k, i, u), :] for u in range(GROUP)], []
            for n in range(modes):
                decay, wave = chunk_mode(fade, k, n), waves[n]
                for u in range(GROUP):
                    wave = decay * wave
                    sums[u] = sums[u] + wave
                ends.append(wave)
            for u in range(GROUP):
                own_li[at_token(k, i, u), :] = sums[u]
            return tuple(ends)

        lax.fori_loop(0, tokens // GROUP, step, start, unroll=2)
        in_copy(5, k).wait()

        def block(b, carry):
            j = k * SUBS + b
            lanes = pl.ds(pl.multiple_of(b * LANES, LANES), LANES)
            conv = own_li[pl.ds(pl.multiple_of(j * pitch, SUBS), tokens), :]
            combined = acc[k, :, lanes] + qli[k, :, lanes].astype(f32) * conv
            acc[k, :, lanes] = combined
            squares_out[...] += combined * combined
            return carry

        lax.fori_loop(0, SUBS, block, 0)

    squares_out[...] = jnp.zeros_like(squares_out)
    for turn in range(chunks + rounds):
        if turn < chunks:
            halo_sent(turn)
            if turn + AHEAD < chunks:
                start_halo(turn + AHEAD)
            medium_and_states(turn)
        for k in range(chunks):
            r = turn - k - 1
            if 0 <= r < rounds:
                take_state(r, k)
                if r + 1 < rounds:
                    send_state(r + 1, k)
        done = turn - rounds
        if 0 <= done < chunks:
            finish_chunk(done)

    sums = squares_out[...]
    for d in range(1, chan_n):
        squares_copy(d).start()
    for d in range(1, chan_n):
        squares_copy(d).wait_recv()
        sums = sums + squares_in[d - 1]
    width = chunks * CHUNK * chan_n
    inverse = lax.rsqrt(jnp.sum(sums, 1, keepdims=True) / width + 1e-06)

    for k in range(chunks):
        outb[k] = (acc[k] * inverse * ngain[:, cols(k)]).astype(bf16)
        pltpu.make_async_copy(outb.at[k], out_h.at[:, cols(k)], out_sem.at[k]).start()

    for k in range(chunks):
        pltpu.make_async_copy(outb.at[k], out_h.at[:, cols(k)], out_sem.at[k]).wait()

        for r in range(rounds):
            for e in range(1, radices[r]):
                sends(r, e, lambda: state_copy(r, e, k).wait_send())

    for d in range(1, chan_n):
        squares_copy(d).wait_send()


def per_device(
    seq_n, chan_n,
    hidden_in, query_mr, key_mr, value_mr, query_li, key_li,
    mr_filter, li_rate, li_residue, norm_gain,
):
    tokens, channels = hidden_in.shape
    groups = mr_filter.shape[1]
    modes = li_rate.shape[0]
    chunks = channels // CHUNK
    radices, _ = stages(seq_n)
    rounds, most = len(radices), max(radices) - 1
    slab = modes * SUBS
    assert seq_n & (seq_n - 1) == 0 and tokens == mr_filter.shape[0] == LANES
    big = pltpu.VMEM((chunks, tokens, CHUNK), bf16)
    dma = pltpu.SemaphoreType.DMA
    return pl.pallas_call(
        functools.partial(mixer_kernel, seq_n, chan_n, chunks, channels // groups),
        out_shape=jax.ShapeDtypeStruct((tokens, channels), bf16),
        in_specs=[pl.BlockSpec(memory_space=pl.ANY)] * 10,
        out_specs=pl.BlockSpec(memory_space=pl.ANY),
        scratch_shapes=[
            big, big, big, big, big, big,
            pltpu.VMEM(mr_filter.shape, bf16),
            pltpu.VMEM(li_rate.shape, f32),
            pltpu.VMEM(li_residue.shape, f32),
            pltpu.VMEM((1, channels), f32),
            big, big, big,
            pltpu.VMEM((groups, tokens), f32),
            pltpu.VMEM((SUBS, tokens, tokens * LANES * groups // channels), bf16),
            pltpu.VMEM((chunks, tokens, CHUNK), f32),
            pltpu.VMEM((channels // LANES * (tokens + SUBS), LANES), f32),
            pltpu.VMEM((channels // LANES * (tokens + SUBS), LANES), f32),
            pltpu.VMEM((chunks * slab, LANES), f32),
            pltpu.VMEM((chunks * slab, LANES), f32),
            pltpu.VMEM((chunks * slab, LANES), f32),
            pltpu.VMEM((chunks, slab, LANES), f32),
            pltpu.VMEM((chunks, slab, LANES), f32),
            pltpu.VMEM((rounds, chunks, slab, LANES), bf16),
            pltpu.VMEM((rounds, most, chunks, slab, LANES), bf16),
            pltpu.VMEM((tokens, LANES), f32),
            pltpu.VMEM((max(chan_n - 1, 1), tokens, LANES), f32),
            dma((6, chunks)),
            dma((4,)),
            dma((chunks,)),
            dma((chunks,)),
            dma((chunks,)),
            dma((rounds, most, chunks)),
            dma((rounds, most, chunks)),
            dma((max(chan_n - 1, 1),)),
            dma((max(chan_n - 1, 1),)),
        ],
        compiler_params=pltpu.CompilerParams(
            collective_id=0, has_side_effects=True, vmem_limit_bytes=63 * 1024 * 1024
        ),
        cost_estimate=pl.CostEstimate(
            flops=4 * tokens * tokens * channels * LANES * groups // channels,
            bytes_accessed=14 * tokens * channels,
            transcendentals=4 * modes * channels,
        ),
        name="hyena_mixers",
    )(
        hidden_in, query_mr, key_mr, value_mr, query_li, key_li,
        mr_filter, li_rate, li_residue, norm_gain.reshape(1, channels),
    )


def solution(mesh):
    seq_n, chan_n = mesh.shape["seq"], mesh.shape["chan"]
    rows = P("seq", "chan")
    by_channel = P(None, "chan")
    in_specs = (rows,) * 6 + (by_channel,) * 3 + (P("chan"),)
    return jax.shard_map(
        functools.partial(per_device, seq_n, chan_n),
        mesh=mesh, in_specs=in_specs, out_specs=rows, check_vma=False,
    )
```
